256 devices in a mesh: dp: 8 (over y, core), fsdp: 32 (over x, z).
Axes of the slice: x: 4, y: 4, z: 8, core: 2. Of those that a mesh axis runs over, the one named last changes fastest.
Arguments:
- activations: bfloat16 [8, 12288, 8192], P('dp', 'fsdp')
- upstream: bfloat16 [8, 12288, 1024], P('dp', 'fsdp')
- momentum: float32 [8, 8192, 1024], P('dp', 'fsdp')
- positions: int32 [8, 128, 16, 32], P(None, 'fsdp'), may hold values from 0 to 4095, as said below
Outputs:
- momentum_out: float32 [8, 8192, 1024], P('dp', 'fsdp')
- update: float32 [8192, 1024], P('fsdp')
The draws below stay inside these ranges and needn't reach their ends.
Inputs may be any that keep to these rules, and one draw needn't show every extreme that they name: For each group and block, 32 distinct positions.
All inputs are finite; a program needn't handle non-finite values.
Results may differ from the reference program's by a relative error of at most 0.0003.
Values may be sent and summed in bfloat16 or wider, within the bound.
A program may use at most 128 MiB of HBM per device.

```python
import math
import jax
import jax.numpy as jnp
from jax import lax

D = 8192
KC = 1024
CH = 64
TOPK = 32
TOK_DEV = 384
TOKENS = 12288
GROUPS = 8


def draw_activations(key, part):
    key = jax.random.fold_in(key, 11)
    first_key, second_key = jax.random.split(key, 2)
    spread_draw = jax.random.uniform(first_key, (D,), jnp.float32)
    feature_scale = 10.0 ** (0.5 * jnp.arange(D, dtype=jnp.float32) / D + 0.5 * spread_draw)
    sample = jnp.clip(jax.random.normal(second_key, (GROUPS, TOKENS, D), jnp.float32), -5.0, 5.0) * feature_scale
    return sample.astype(jnp.bfloat16)


def draw_upstream(key, part):
    key = jax.random.fold_in(key, 12)
    first_key, second_key = jax.random.split(key, 2)
    column_scale = 10.0 ** jax.random.uniform(first_key, (KC,), jnp.float32)
    sample = jnp.clip(jax.random.normal(second_key, (GROUPS, TOKENS, KC), jnp.float32), -5.0, 5.0) * column_scale
    return (sample * (1.0 / math.sqrt(TOKENS))).astype(jnp.bfloat16)


def draw_momentum(key, part):
    key = jax.random.fold_in(key, 14)
    first_key, second_key, third_key = jax.random.split(key, 3)
    row_rough = jax.random.uniform(first_key, (D, 1), jnp.float32, 0.6, 1.4)
    column_rough = jax.random.uniform(third_key, (1, KC), jnp.float32, 0.7, 1.3)
    row_place = jnp.arange(D, dtype=jnp.float32)[:, None] / D
    base_draw = jnp.clip(jax.random.normal(second_key, (GROUPS, D, KC), jnp.float32), -5.0, 5.0)
    row_scale = 10.0 ** (0.4 * row_place)
    return base_draw * (row_scale * row_rough * column_rough)


def draw_positions(key, part):
    key = jax.random.fold_in(key, 13)
    scores = jax.random.randint(key, (GROUPS, D // CH, KC // CH, CH * CH), 0, 2 ** 30)
    ordering = jnp.argsort(scores, axis=-1, stable=True)
    return ordering[..., :TOPK].astype(jnp.int32)


def setup_inputs(seed: int = 0) -> dict:
    key_of = jax.random.split(jax.random.key(seed), 5)
    activations = draw_activations(jax.random.fold_in(key_of[4], 71), 0)
    upstream = draw_upstream(jax.random.fold_in(key_of[4], 71), 0)
    momentum = draw_momentum(jax.random.fold_in(key_of[4], 71), 0)
    positions = draw_positions(jax.random.fold_in(key_of[4], 71), 0)
    return dict(activations=activations, upstream=upstream, momentum=momentum, positions=positions)


beta_rate = 0.999
clip_rms = 1.0
sharpness = 0.5
small_eps = 1e-06
exact_mode = lax.Precision.HIGHEST

def dct_table(block_size):
    frequency = jnp.arange(block_size, dtype=jnp.float32)[:, None]
    sample_at = jnp.arange(block_size, dtype=jnp.float32)[None, :]
    scaling = jnp.where(frequency == 0.0, math.sqrt(1.0 / block_size), math.sqrt(2.0 / block_size))
    return scaling * jnp.cos(math.pi * (2.0 * sample_at + 1.0) * frequency / (2.0 * block_size))

def paired(cosines):
    zeroes = jnp.zeros_like(cosines)
    return jnp.concatenate([jnp.concatenate([cosines, zeroes], 1), jnp.concatenate([zeroes, cosines], 1)], 0)

def forward(matrix, cosines, paired_cos):
    height, breadth = matrix.shape
    block_size = cosines.shape[0]
    section = jnp.einsum('ij,ajc->aic', cosines, matrix.reshape(height // block_size, block_size, breadth), precision=exact_mode)
    result = jnp.einsum('rbk,lk->rbl', section.reshape(height, breadth // (2 * block_size), 2 * block_size), paired_cos, precision=exact_mode)
    return result.reshape(height, breadth)

def inverse(matrix, cosines, paired_cos):
    height, breadth = matrix.shape
    block_size = cosines.shape[0]
    section = jnp.einsum('ji,ajc->aic', cosines, matrix.reshape(height // block_size, block_size, breadth), precision=exact_mode)
    result = jnp.einsum('rbk,kl->rbl', section.reshape(height, breadth // (2 * block_size), 2 * block_size), paired_cos, precision=exact_mode)
    return result.reshape(height, breadth)

def to_blocks(matrix, block_size):
    height, breadth = matrix.shape
    shaped = matrix.reshape(height // block_size, block_size, breadth // block_size, block_size)
    return shaped.transpose(0, 2, 1, 3).reshape(height // block_size * (breadth // block_size), block_size * block_size)

def place_values(values, chosen_at, height, breadth, block_size):
    number = values.shape[0]
    block_ids = jnp.arange(number, dtype=jnp.int32)[:, None]
    dense = jnp.zeros((number, block_size * block_size), jnp.float32).at[block_ids, chosen_at].add(values)
    shaped = dense.reshape(height // block_size, breadth // block_size, block_size, block_size)
    return shaped.transpose(0, 2, 1, 3).reshape(height, breadth)

def add_part(running, shard_pair):
    product = jnp.dot(shard_pair[0].T, shard_pair[1], preferred_element_type=jnp.float32)
    return (running + product, None)

def reference(activations, upstream, momentum, positions):
    cosines = dct_table(CH)
    paired_cos = paired(cosines)
    limit = clip_rms * math.sqrt(D * KC)
    blocks = D // CH * (KC // CH)
    combined = jnp.zeros((D, KC), jnp.float32)
    results = []
    for group_id in range(GROUPS):
        inputs = activations[group_id].reshape(TOKENS // TOK_DEV, TOK_DEV, D)
        cotangent = upstream[group_id].reshape(TOKENS // TOK_DEV, TOK_DEV, KC)
        gradient, _ = lax.scan(add_part, jnp.zeros((D, KC), jnp.float32), (inputs, cotangent))
        grad_length = jnp.sqrt(jnp.sum(gradient * gradient))
        factor = limit / jnp.maximum(grad_length, limit)
        blended = beta_rate * momentum[group_id] + factor * gradient
        spectrum = forward(blended, cosines, paired_cos)
        chosen_at = positions[group_id].reshape(blocks, TOPK)
        chosen = jnp.take_along_axis(to_blocks(spectrum, CH), chosen_at, axis=1)
        own_part = inverse(place_values(chosen, chosen_at, D, KC, CH), cosines, paired_cos)
        results.append(blended - own_part)
        combined = combined + own_part
    combined = combined / GROUPS
    spread = jnp.sqrt(jnp.sum(combined * combined) / (D * KC) + small_eps)
    update = jnp.tanh(combined / (sharpness * spread))
    return (jnp.stack(results), update)
```

```python
import math

import jax
import jax.numpy as jnp
import ml_dtypes
import numpy as np
from jax import lax
from jax.experimental import pallas as pl
from jax.experimental.pallas import tpu as pltpu
from jax.sharding import PartitionSpec as P

D = 8192
KC = 1024
CH = 64
TOK = 384
GROUPS = 8
NX = 4
NZ = 8
ROWS = 256
HALF = 128
SPAN = NZ * ROWS
AHEAD = 3
LIMIT = math.sqrt(D * KC)
MESH = pl.DeviceIdType.MESH
F32 = jnp.float32
BF16 = jnp.bfloat16
NT = (((1,), (1,)), ((), ()))
TN = (((0,), (0,)), ((), ()))


def cosine_parts():
    k = np.arange(CH, dtype=np.float64)[:, None]
    n = np.arange(CH, dtype=np.float64)[None, :]
    s = np.where(k == 0, math.sqrt(1.0 / CH), math.sqrt(2.0 / CH))
    c = s * np.cos(math.pi * (2.0 * n + 1.0) * k / (2.0 * CH))
    wide = np.kron(np.eye(4), c)
    high = wide.astype(ml_dtypes.bfloat16)
    low = (wide - high.astype(np.float64)).astype(ml_dtypes.bfloat16)
    return np.stack([high, low, high.T, low.T])


def split(x):
    high = x.astype(BF16)
    return high, (x - high.astype(F32)).astype(BF16)


def dot(a, b):
    return jnp.dot(a, b, preferred_element_type=F32)


def kernel(a_ref, u_ref, m_ref, pos_ref, cos_ref, mom_ref, upd_ref,
           ra, ua, at, part, sbuf, rbuf, ssc, rsc, grad, xg, xm, mask, mom, own, cone,
           vals, vg, vm, norm, spread, asend, arecv, usend, urecv, zsend, zrecv, csend, crecv,
           vsend, vrecv, nsend, nrecv, lsem):
    d = lax.axis_index("dp")
    f = lax.axis_index("fsdp")
    x = f // NZ
    z = f % NZ

    def xpeer(dx):
        return {"dp": d, "fsdp": (x + dx) % NX * NZ + z}

    def zpeer(dz):
        return {"dp": d, "fsdp": x * NZ + (z + dz + NZ) % NZ}

    def gpeer(i):
        return {"dp": (d + i) % GROUPS, "fsdp": f}

    def fpeer(i):
        return {"dp": d, "fsdp": (f + i) % (NX * NZ)}

    barrier = pltpu.get_barrier_semaphore()
    peers = [xpeer(i) for i in range(1, NX)] + [zpeer(1), zpeer(-1)]
    peers += [gpeer(i) for i in range(1, GROUPS)]
    for peer in peers:
        pl.semaphore_signal(barrier, inc=1, device_id=peer, device_id_type=MESH)

    def chunk(h, s):
        return (z - 1 - s + 2 * NZ) % NZ if h == 0 else (z + 1 + s) % NZ

    def a_cols(dx, h, s):
        start = (x + dx) % NX * SPAN + chunk(h, s) * ROWS + h * HALF
        return pl.ds(pl.multiple_of(start, HALF), HALF)

    def a_copy(dx, h, s):
        return pltpu.make_async_remote_copy(
            src_ref=a_ref.at[0, :, a_cols(dx, h, s)],
            dst_ref=ra.at[s, dx, :, pl.ds(h * HALF, HALF)],
            send_sem=asend.at[dx, h, s], recv_sem=arecv.at[dx, h, s],
            device_id=xpeer(dx), device_id_type=MESH)

    def a_local(h, s):
        return pltpu.make_async_copy(
            a_ref.at[0, :, a_cols(0, h, s)], ra.at[s, 0, :, pl.ds(h * HALF, HALF)], arecv.at[0, h, s])

    def u_copy(dx):
        return pltpu.make_async_remote_copy(
            src_ref=u_ref.at[0], dst_ref=ua.at[dx], send_sem=usend.at[dx], recv_sem=urecv.at[dx],
            device_id=xpeer(dx), device_id_type=MESH)

    def z_copies(h, s):
        peer = zpeer(1 if h == 0 else -1)
        return (
            pltpu.make_async_remote_copy(
                src_ref=sbuf.at[h, s], dst_ref=rbuf.at[h, s], send_sem=zsend.at[h, s],
                recv_sem=zrecv.at[h, s], device_id=peer, device_id_type=MESH),
            pltpu.make_async_remote_copy(
                src_ref=ssc.at[h, s], dst_ref=rsc.at[h, s], send_sem=csend.at[h, s],
                recv_sem=crecv.at[h, s], device_id=peer, device_id_type=MESH))

    u_local = pltpu.make_async_copy(u_ref.at[0], ua.at[0], urecv.at[0])
    u_local.start()
    m_local = pltpu.make_async_copy(m_ref.at[0], mom, lsem.at[0])
    m_local.start()

    def start_local(s, c):
        for h in range(2):
            a_local(h, s).start()
        return c

    lax.fori_loop(0, NZ, start_local, 0)

    pl.semaphore_wait(barrier, len(peers))

    for dx in range(1, NX):
        u_copy(dx).start()

    def start_a(s):
        for h in range(2):
            for dx in (1, 3, 2):
                a_copy(dx, h, s).start()

    def start_first(s, c):
        start_a(s)
        return c

    lax.fori_loop(0, AHEAD, start_first, 0)

    def one_hot_columns(q, c):
        wide = lax.broadcasted_iota(jnp.int32, (ROWS, HALF), 0)
        lane = lax.broadcasted_iota(jnp.int32, (1, HALF), 1)
        for g in range(GROUPS):
            p = pos_ref[g, pl.ds(q, 1), :]
            col = (p & (CH - 1)) + (lane >> 5) * CH
            cone[q, :, g * HALF:(g + 1) * HALF] = jnp.where(wide == col, 1.0, 0.0).astype(BF16)
        return c

    lax.fori_loop(0, 16, one_hot_columns, 0)

    def quad(ref, q):
        rows = pl.ds(pl.multiple_of(q // 4 * CH, CH), CH)
        return ref.at[rows, pl.ds(pl.multiple_of(q % 4 * ROWS, ROWS), ROWS)]

    def own_columns(q):
        return cone[q, :, pl.ds(pl.multiple_of(d * HALF, HALF), HALF)]

    def own_rows(q):
        tall = lax.broadcasted_iota(jnp.int32, (CH, HALF), 0)
        return jnp.where(tall == (pos_ref[d, pl.ds(q, 1), :] >> 6), 1.0, 0.0).astype(BF16)

    def build_mask(q, c):
        quad(mask, q)[...] = lax.dot_general(own_rows(q), own_columns(q), NT, preferred_element_type=F32)
        return c

    lax.fori_loop(0, 16, build_mask, 0)

    def transform(src, dst, left, right):
        def body(j, c):
            cols = pl.ds(pl.multiple_of(j * ROWS, ROWS), ROWS)
            h, l = split(src[:, cols])
            y = dot(cos_ref[left], h) + dot(cos_ref[left], l) + dot(cos_ref[left + 1], h)
            h, l = split(y)
            dst[:, cols] = dot(h, cos_ref[right]) + dot(l, cos_ref[right]) + dot(h, cos_ref[right + 1])
            return c

        lax.fori_loop(0, KC // ROWS, body, 0)

    def gather(src, dst):
        def body(q, c):
            h, l = split(quad(src, q)[...])
            r = own_rows(q)
            t = (lax.dot_general(h, r, TN, preferred_element_type=F32)
                 + lax.dot_general(l, r, TN, preferred_element_type=F32))
            dst[pl.ds(q, 1), :] = jnp.sum(t * own_columns(q).astype(F32), axis=0, keepdims=True)
            return c

        lax.fori_loop(0, 16, body, 0)

    m_local.wait()
    transform(mom, xm, 0, 2)
    gather(xm, vm)

    u_local.wait()
    for dx in range(1, NX):
        u_copy(dx).wait_recv()

    def product(s):
        for h in range(2):
            a_local(h, s).wait()
            for dx in range(1, NX):
                a_copy(dx, h, s).wait_recv()
        for dx in range(NX):
            at[:, dx * TOK:(dx + 1) * TOK] = ra[s, dx].T

        def body(j, c):
            cols = pl.ds(pl.multiple_of(j * ROWS, ROWS), ROWS)
            total = dot(at[:, 0:TOK], ua[0, :, cols])
            for dx in range(1, NX):
                total += dot(at[:, dx * TOK:(dx + 1) * TOK], ua[dx, :, cols])
            part[:, cols] = total
            return c

        lax.fori_loop(0, KC // ROWS, body, 0)

    def reduce_step(h, s, first, last):
        if not first:
            for copy in z_copies(h, s - 1):
                copy.wait_recv()

        def body(j, c):
            cols = pl.ds(pl.multiple_of(j * HALF, HALF), HALF)
            v = part[h * HALF:(h + 1) * HALF, cols]
            if not first:
                v += rbuf[h, s - 1, :, cols].astype(F32) * rsc[h, s - 1, pl.ds(j, 1), :]
            if last:
                grad[h * HALF:(h + 1) * HALF, cols] = v
            else:
                top = jnp.maximum(jnp.max(jnp.abs(v), axis=0, keepdims=True), 1e-30)
                ssc[h, s, pl.ds(j, 1), :] = top * (1.0 / 32767.0)
                q = lax.round(v * (32767.0 / top), lax.RoundingMethod.TO_NEAREST_EVEN)
                sbuf[h, s, :, cols] = q.astype(jnp.int32).astype(jnp.int16)
            return c

        lax.fori_loop(0, KC // HALF, body, 0)
        if not last:
            for copy in z_copies(h, s):
                copy.start()

    def full_step(s, first, last):
        if first:
            start_a(AHEAD)
        elif not last:
            @pl.when(s + AHEAD < NZ)
            def _():
                start_a(s + AHEAD)
        product(s)
        for h in range(2):
            reduce_step(h, s, first, last)

    full_step(0, True, False)

    def middle(s, c):
        full_step(s, False, False)
        return c

    lax.fori_loop(1, NZ - 1, middle, 0)
    full_step(NZ - 1, False, True)

    def share(e, buf):
        def go(i, c):
            pltpu.make_async_remote_copy(
                src_ref=buf.at[f], dst_ref=buf.at[f], send_sem=nsend.at[e, i], recv_sem=nrecv.at[e, i],
                device_id=fpeer(i), device_id_type=MESH).start()
            return c

        lax.fori_loop(1, NX * NZ, go, 0)

    def shared(e, buf):
        def go(i, c):
            pltpu.make_async_remote_copy(
                src_ref=buf.at[f], dst_ref=buf.at[(f - i + NX * NZ) % (NX * NZ)],
                send_sem=nsend.at[e, i], recv_sem=nrecv.at[e, i],
                device_id=fpeer(i), device_id_type=MESH).wait_recv()
            return c

        lax.fori_loop(1, NX * NZ, go, 0)
        return jnp.sum(jnp.sum(buf[...], axis=0), keepdims=True)

    def squares(ref):
        def body(i, acc):
            v = ref[pl.ds(pl.multiple_of(i * 8, 8), 8), :]
            return acc + v * v

        acc = lax.fori_loop(0, ROWS // 8, body, jnp.zeros((8, KC), F32))
        total = acc[:, 0:HALF]
        for j in range(1, KC // HALF):
            total += acc[:, j * HALF:(j + 1) * HALF]
        return jnp.sum(total, axis=0, keepdims=True)

    norm[f] = squares(grad)
    share(0, norm)
    transform(grad, xg, 0, 2)
    gather(xg, vg)
    total = shared(0, norm)
    factor = LIMIT / jnp.maximum(jnp.sqrt(total), LIMIT)

    vals[d] = 0.999 * vm[...] + factor * vg[...]

    def v_copy(i, target):
        return pltpu.make_async_remote_copy(
            src_ref=vals.at[d], dst_ref=vals.at[target], send_sem=vsend.at[i], recv_sem=vrecv.at[i],
            device_id=gpeer(i), device_id_type=MESH)

    for i in range(1, GROUPS):
        v_copy(i, d).start()

    xg[...] = mask[...] * (0.999 * xm[...] + factor * xg[...])
    transform(xg, own, 2, 0)
    mom[...] = 0.999 * mom[...] + factor * grad[...] - own[...]
    mom_out = pltpu.make_async_copy(mom, mom_ref.at[0], lsem.at[0])
    mom_out.start()

    for i in range(1, GROUPS):
        v_copy(i, (d - i + GROUPS) % GROUPS).wait_recv()

    def scatter(q, c):
        tall = lax.broadcasted_iota(jnp.int32, (CH, HALF), 0)
        pieces = []
        for g in range(GROUPS):
            hit = tall == (pos_ref[g, pl.ds(q, 1), :] >> 6)
            pieces.append(jnp.where(hit, vals[g, pl.ds(q, 1), :], 0.0))
        h, l = split(jnp.concatenate(pieces, axis=1))
        both = lax.dot_general(jnp.concatenate([h, l], axis=0), cone[q], NT, preferred_element_type=F32)
        quad(xm, q)[...] = (both[0:CH] + both[CH:2 * CH]) * (1.0 / GROUPS)
        return c

    lax.fori_loop(0, 16, scatter, 0)
    spread[f] = squares(xm)
    share(1, spread)
    transform(xm, own, 2, 0)
    width = jnp.sqrt(shared(1, spread) / (D * KC) + 1e-6)
    own[...] = jnp.tanh(own[...] / (0.5 * width))
    upd_out = pltpu.make_async_copy(own, upd_ref, lsem.at[1])
    upd_out.start()

    def a_sent(s, c):
        for h in range(2):
            for dx in range(1, NX):
                a_copy(dx, h, s).wait_send()
        return c

    def z_sent(s, c):
        for h in range(2):
            for copy in z_copies(h, s):
                copy.wait_send()
        return c

    def n_sent(i, c):
        for e, buf in enumerate((norm, spread)):
            pltpu.make_async_remote_copy(
                src_ref=buf.at[f], dst_ref=buf.at[f], send_sem=nsend.at[e, i], recv_sem=nrecv.at[e, i],
                device_id=fpeer(i), device_id_type=MESH).wait_send()
        return c

    lax.fori_loop(0, NZ, a_sent, 0)
    lax.fori_loop(0, NZ - 1, z_sent, 0)
    lax.fori_loop(1, NX * NZ, n_sent, 0)
    for dx in range(1, NX):
        u_copy(dx).wait_send()
    for i in range(1, GROUPS):
        v_copy(i, d).wait_send()
    mom_out.wait()
    upd_out.wait()


def local(activations, upstream, momentum, positions):
    picked = positions.reshape(GROUPS, 16, HALF)
    dma = pltpu.SemaphoreType.DMA
    hbm = pl.BlockSpec(memory_space=pl.ANY)
    vmem = pl.BlockSpec(memory_space=pltpu.VMEM)
    return pl.pallas_call(
        kernel,
        out_shape=(
            jax.ShapeDtypeStruct((1, ROWS, KC), F32),
            jax.ShapeDtypeStruct((ROWS, KC), F32),
        ),
        in_specs=[hbm, hbm, hbm, vmem, vmem],
        out_specs=(hbm, hbm),
        scratch_shapes=[
            pltpu.VMEM((NZ, NX, TOK, 2 * HALF), BF16),
            pltpu.VMEM((NX, TOK, KC), BF16),
            pltpu.VMEM((ROWS, NX * TOK), BF16),
            pltpu.VMEM((ROWS, KC), F32),
            pltpu.VMEM((2, NZ - 1, HALF, KC), jnp.int16),
            pltpu.VMEM((2, NZ - 1, HALF, KC), jnp.int16),
            pltpu.VMEM((2, NZ - 1, 8, HALF), F32),
            pltpu.VMEM((2, NZ - 1, 8, HALF), F32),
            pltpu.VMEM((ROWS, KC), F32),
            pltpu.VMEM((ROWS, KC), F32),
            pltpu.VMEM((ROWS, KC), F32),
            pltpu.VMEM((ROWS, KC), F32),
            pltpu.VMEM((ROWS, KC), F32),
            pltpu.VMEM((ROWS, KC), F32),
            pltpu.VMEM((16, ROWS, GROUPS * HALF), BF16),
            pltpu.VMEM((GROUPS, 16, HALF), F32),
            pltpu.VMEM((16, HALF), F32),
            pltpu.VMEM((16, HALF), F32),
            pltpu.VMEM((NX * NZ, 1, HALF), F32),
            pltpu.VMEM((NX * NZ, 1, HALF), F32),
            dma((NX, 2, NZ)),
            dma((NX, 2, NZ)),
            dma((NX,)),
            dma((NX,)),
            dma((2, NZ - 1)),
            dma((2, NZ - 1)),
            dma((2, NZ - 1)),
            dma((2, NZ - 1)),
            dma((GROUPS,)),
            dma((GROUPS,)),
            dma((2, NX * NZ)),
            dma((2, NX * NZ)),
            dma((2,)),
        ],
        compiler_params=pltpu.CompilerParams(
            collective_id=0, has_side_effects=True, vmem_limit_bytes=56 * 2**20),
        cost_estimate=pl.CostEstimate(flops=7 * 10**9, bytes_accessed=12 * 10**6, transcendentals=0),
    )(activations, upstream, momentum, picked, jnp.asarray(cosine_parts()))


def solution(mesh):
    placed = (
        P("dp", "fsdp", None),
        P("dp", "fsdp", None),
        P("dp", "fsdp", None),
        P(None, "fsdp", None, None),
    )
    return jax.shard_map(
        local,
        mesh=mesh,
        in_specs=placed,
        out_specs=(P("dp", "fsdp", None), P("fsdp", None)),
        check_vma=False,
    )
```

```python
import math

import jax
import jax.numpy as jnp
import ml_dtypes
import numpy as np
from jax import lax
from jax.experimental import pallas as pl
from jax.experimental.pallas import tpu as pltpu
from jax.sharding import PartitionSpec as P

D = 8192
KC = 1024
CH = 64
TOK = 384
GROUPS = 8
NX = 4
NZ = 8
ROWS = 256
HALF = 128
SPAN = NZ * ROWS
AHEAD_C = 4
AHEAD_A = 3
LAG = 1
NB = 1
STRIP = 64
WIDE = KC // NB
LIMIT = math.sqrt(D * KC)
MESH = pl.DeviceIdType.MESH
F32 = jnp.float32
BF16 = jnp.bfloat16
NT = (((1,), (1,)), ((), ()))
TN = (((0,), (0,)), ((), ()))


def cosine_parts():
    k = np.arange(CH, dtype=np.float64)[:, None]
    n = np.arange(CH, dtype=np.float64)[None, :]
    s = np.where(k == 0, math.sqrt(1.0 / CH), math.sqrt(2.0 / CH))
    c = s * np.cos(math.pi * (2.0 * n + 1.0) * k / (2.0 * CH))
    wide = np.kron(np.eye(4), c)
    high = wide.astype(ml_dtypes.bfloat16)
    low = (wide - high.astype(np.float64)).astype(ml_dtypes.bfloat16)
    return np.stack([high, low, high.T, low.T])


def split(x):
    high = x.astype(BF16)
    return high, (x - high.astype(F32)).astype(BF16)


def dot(a, b):
    return jnp.dot(a, b, preferred_element_type=F32)


def kernel(a_ref, u_ref, m_ref, raw_ref, cos_hbm, mom_ref, upd_ref, width_ref,
           pos_ref, cos_ref, raw,
           ra, rc, ua, ata, atc, part, sbuf, rbuf, ssc, rsc, fbuf, fsc, grad, xg, xm, mask, mom, own, cone,
           vals, vg, vm, norm, spread, asend, arecv, bsend, brecv, blocal, usend, urecv, psend, precv,
           zsend, zrecv, csend, crecv, fsend, frecv, vsend, vrecv, nsend, nrecv, lsem):
    d = lax.axis_index("dp")
    f = lax.axis_index("fsdp")
    x = f // NZ
    z = f % NZ

    core = d % 2
    way = 1 - 2 * core

    def flip(v, j):
        if j == 1:
            return v + 1 - 2 * (v % 2)
        return (v + 2) % NX if j == 2 else NX - 1 - v

    def pick(v, p):
        return flip(v, 1) + p * (flip(v, 3) - flip(v, 1))

    def at_x(v):
        return {"dp": d, "fsdp": v * NZ + z}

    def xpeer(j):
        return at_x(flip(x, j))

    def zpeer(dz):
        return {"dp": d, "fsdp": x * NZ + (z + dz + NZ) % NZ}

    def gpeer(i):
        return {"dp": (d + i) % GROUPS, "fsdp": f}

    def fpeer(i):
        return {"dp": d, "fsdp": (f + i) % (NX * NZ)}

    barrier = pltpu.get_barrier_semaphore()
    peers = [xpeer(i) for i in range(1, NX)] + [zpeer(-way)]
    peers += [gpeer(i) for i in range(1, GROUPS)]
    for peer in peers:
        pl.semaphore_signal(barrier, inc=1, device_id=peer, device_id_type=MESH)

    def chunk(s):
        return (z - way * (1 + s) + 2 * NZ) % NZ

    def pairing(s):
        return (chunk(s) + core) % 2

    def cols(quarter, s, h):
        start = quarter * SPAN + chunk(s) * ROWS + h * HALF
        return pl.ds(pl.multiple_of(start, HALF), HALF)

    def a_copy(j, s):
        return pltpu.make_async_remote_copy(
            src_ref=a_ref.at[0, :, cols(flip(x, j), s, 0)], dst_ref=ra.at[s, j],
            send_sem=asend.at[j, s], recv_sem=arecv.at[j, s], device_id=xpeer(j), device_id_type=MESH)

    def a_local(s):
        return pltpu.make_async_copy(a_ref.at[0, :, cols(x, s, 0)], ra.at[s, 0], arecv.at[0, s])

    def c_copy(q, s):
        p = pairing(s)
        near = pick(x, p)
        quarter = near if q == 1 else pick(near, 1 - p)
        return pltpu.make_async_remote_copy(
            src_ref=a_ref.at[0, :, cols(quarter, s, 1)], dst_ref=rc.at[s, 1, q],
            send_sem=bsend.at[q, s], recv_sem=brecv.at[q, s], device_id=at_x(near), device_id_type=MESH)

    def c_local(q, s):
        quarter = x if q == 1 else pick(x, 1 - pairing(s))
        return pltpu.make_async_copy(a_ref.at[0, :, cols(quarter, s, 1)], rc.at[s, 0, q], blocal.at[q, s])

    def u_copy(j):
        return pltpu.make_async_remote_copy(
            src_ref=u_ref.at[0], dst_ref=ua.at[j], send_sem=usend.at[j], recv_sem=urecv.at[j],
            device_id=xpeer(j), device_id_type=MESH)

    def u_pass(j):
        rows = pl.ds(0, TOK // 2) if j == 1 else pl.ds(TOK // 2, TOK // 2)
        return pltpu.make_async_remote_copy(
            src_ref=ua.at[4 - j, rows], dst_ref=ua.at[2, rows], send_sem=psend.at[j], recv_sem=precv.at[j],
            device_id=xpeer(j), device_id_type=MESH)

    def pair_of(data, scale, device):
        return [
            pltpu.make_async_remote_copy(
                src_ref=src, dst_ref=dst, send_sem=ss, recv_sem=rs, device_id=device, device_id_type=MESH)
            for src, dst, ss, rs in (data, scale)]

    def z_copies(w, b, s):
        return pair_of(
            (sbuf.at[w, b, s], rbuf.at[w, b, s + 1], zsend.at[w, b, s], zrecv.at[w, b, s + 1]),
            (ssc.at[w, b, s], rsc.at[w, b, s + 1], csend.at[w, b, s], crecv.at[w, b, s + 1]),
            zpeer(way))

    def far_copies(b):
        return pair_of(
            (fbuf.at[0, b], fbuf.at[1, b], fsend.at[0, b], frecv.at[0, b]),
            (fsc.at[0, b], fsc.at[1, b], fsend.at[1, b], frecv.at[1, b]),
            at_x(pick(x, 1 - pairing(NZ - 1))))

    u_local = pltpu.make_async_copy(u_ref.at[0], ua.at[0], urecv.at[0])
    u_local.start()
    m_local = pltpu.make_async_copy(m_ref.at[0], mom, lsem.at[0])
    m_local.start()

    cos_local = pltpu.make_async_copy(cos_hbm, cos_ref, lsem.at[1])
    cos_local.start()
    raw_local = pltpu.make_async_copy(raw_ref, raw, lsem.at[2])
    raw_local.start()

    def start_local(s, c):
        for q in range(2):
            c_local(q, s).start()
        a_local(s).start()
        return c

    lax.fori_loop(0, NZ, start_local, 0)

    pl.semaphore_wait(barrier, len(peers))

    for j in (1, 3):
        u_copy(j).start()

    def start_c(s, c):
        for q in range(2):
            c_copy(q, s).start()
        return c

    def start_a(s, c):
        for j in (1, 3, 2):
            a_copy(j, s).start()
        return c

    lax.fori_loop(0, AHEAD_C, start_c, 0)

    def clear(i, c):
        for w in range(3):
            for b in range(NB):
                rbuf[w, b, 0, pl.ds(pl.multiple_of(i * 16, 16), 16), :] = jnp.zeros((16, WIDE), jnp.int16)
        return c

    lax.fori_loop(0, HALF // 16, clear, 0)
    for w in range(3):
        for b in range(NB):
            rsc[w, b, 0] = jnp.zeros((8, HALF), F32)

    raw_local.wait()
    for g in range(GROUPS):
        for a in range(4):
            pos_ref[g, a * 4:(a + 1) * 4, :] = jnp.concatenate(
                [raw[g, a, pl.ds(m, 4, stride=4), :] for m in range(4)], axis=1)

    def one_hot_columns(q, c):
        wide = lax.broadcasted_iota(jnp.int32, (ROWS, HALF), 0)
        lane = lax.broadcasted_iota(jnp.int32, (1, HALF), 1)
        for g in range(GROUPS):
            p = pos_ref[g, pl.ds(q, 1), :]
            col = (p & (CH - 1)) + (lane >> 5) * CH
            cone[q, :, g * HALF:(g + 1) * HALF] = jnp.where(wide == col, 1.0, 0.0).astype(BF16)
        return c

    lax.fori_loop(0, 16, one_hot_columns, 0)

    def quad(ref, q):
        rows = pl.ds(pl.multiple_of(q // 4 * CH, CH), CH)
        return ref.at[rows, pl.ds(pl.multiple_of(q % 4 * ROWS, ROWS), ROWS)]

    def own_columns(q):
        return cone[q, :, pl.ds(pl.multiple_of(d * HALF, HALF), HALF)]

    def own_rows(q):
        tall = lax.broadcasted_iota(jnp.int32, (CH, HALF), 0)
        return jnp.where(tall == (pos_ref[d, pl.ds(q, 1), :] >> 6), 1.0, 0.0).astype(BF16)

    def build_mask(q, c):
        quad(mask, q)[...] = lax.dot_general(own_rows(q), own_columns(q), NT, preferred_element_type=F32)
        return c

    lax.fori_loop(0, 16, build_mask, 0)

    def transform(src, dst, left, right):
        def body(j, c):
            at_cols = pl.ds(pl.multiple_of(j * ROWS, ROWS), ROWS)
            h, l = split(src[:, at_cols])
            y = dot(cos_ref[left], h) + dot(cos_ref[left], l) + dot(cos_ref[left + 1], h)
            h, l = split(y)
            dst[:, at_cols] = dot(h, cos_ref[right]) + dot(l, cos_ref[right]) + dot(h, cos_ref[right + 1])
            return c

        lax.fori_loop(0, KC // ROWS, body, 0)

    def gather(src, dst):
        def body(q, c):
            h, l = split(quad(src, q)[...])
            r = own_rows(q)
            t = (lax.dot_general(h, r, TN, preferred_element_type=F32)
                 + lax.dot_general(l, r, TN, preferred_element_type=F32))
            dst[pl.ds(q, 1), :] = jnp.sum(t * own_columns(q).astype(F32), axis=0, keepdims=True)
            return c

        lax.fori_loop(0, 16, body, 0)

    m_local.wait()
    cos_local.wait()
    transform(mom, xm, 0, 2)
    gather(xm, vm)

    u_local.wait()
    for j in (1, 3):
        u_copy(j).wait_recv()
    for j in (1, 3):
        u_pass(j).start()
    lax.fori_loop(0, AHEAD_A, start_a, 0)

    def product_c(s):
        for q in range(2):
            c_local(q, s).wait()
            c_copy(q, s).wait_recv()
        for q in range(2):
            for k in range(2):
                atc[q * HALF:(q + 1) * HALF, k * TOK:(k + 1) * TOK] = rc[s, k, q].T
        near = 1 + 2 * pairing(s)

        def body(j, c):
            here = pl.ds(pl.multiple_of(j * ROWS, ROWS), ROWS)
            both = jnp.concatenate([ua[0, :, here], ua[near, :, here]], axis=0)
            part[0:ROWS, here] = dot(atc[...], both)
            return c

        lax.fori_loop(0, KC // ROWS, body, 0)

    def product_a(s):
        a_local(s).wait()
        for j in range(1, NX):
            a_copy(j, s).wait_recv()
        for j in range(NX):
            ata[:, j * TOK:(j + 1) * TOK] = ra[s, j].T

        def body(j, c):
            here = pl.ds(pl.multiple_of(j * ROWS, ROWS), ROWS)
            part[ROWS:ROWS + HALF, here] = dot(ata[...], ua[:, :, here].reshape(NX * TOK, ROWS))
            return c

        lax.fori_loop(0, KC // ROWS, body, 0)

    def encode(v, codes, scales, j, here):
        top = jnp.maximum(jnp.max(jnp.abs(v), axis=0, keepdims=True), 1e-30)
        scales[pl.ds(j, 1), :] = top * (1.0 / 32767.0)
        code = lax.round(v * (32767.0 / top), lax.RoundingMethod.TO_NEAREST_EVEN)
        codes[:, here] = code.astype(jnp.int32).astype(jnp.int16)

    def reduce_step(w, s, last):
        for b in range(NB):
            @pl.when(s > 0)
            def _():
                for copy in z_copies(w, b, s - 1):
                    copy.wait_recv()

            def body(j, c):
                here = pl.ds(pl.multiple_of(j * HALF, HALF), HALF)
                there = pl.ds(pl.multiple_of(b * WIDE + j * HALF, HALF), HALF)
                v = part[w * HALF:(w + 1) * HALF, there]
                v += rbuf[w, b, s, :, here].astype(F32) * rsc[w, b, s, pl.ds(j, 1), :]
                if not last:
                    encode(v, sbuf.at[w, b, s], ssc.at[w, b, s], j, here)
                elif w == 0:
                    encode(v, fbuf.at[0, b], fsc.at[0, b], j, here)
                else:
                    top = HALF * (w % 2)
                    grad[top:top + HALF, there] = v
                return c

            lax.fori_loop(0, WIDE // HALF, body, 0)
            if not last:
                for copy in z_copies(w, b, s):
                    copy.start()
            elif w == 0:
                for copy in far_copies(b):
                    copy.start()

    def step_c(s, last):
        @pl.when(s + AHEAD_C < NZ)
        def _():
            start_c(s + AHEAD_C, 0)
        product_c(s)
        reduce_step(0, s, last)
        reduce_step(1, s, last)

    def step_a(s, last):
        @pl.when(s + AHEAD_A < NZ)
        def _():
            start_a(s + AHEAD_A, 0)
        product_a(s)
        reduce_step(2, s, last)

    def only_c(t, c):
        step_c(t, False)
        return c

    def mixed(t, c):
        step_c(t, False)
        step_a(t - LAG, False)
        return c

    def only_a(t, c):
        step_a(t - LAG, False)
        return c

    lax.fori_loop(0, LAG, only_c, 0)
    for j in (1, 3):
        u_pass(j).wait_recv()
    lax.fori_loop(LAG, NZ - 1, mixed, 0)
    step_c(NZ - 1, True)
    lax.fori_loop(NZ - 1, NZ - 1 + LAG, only_a, 0)
    step_a(NZ - 1, True)

    for b in range(NB):
        for copy in far_copies(b):
            copy.wait_recv()

        def add_far(j, c):
            here = pl.ds(pl.multiple_of(j * HALF, HALF), HALF)
            there = pl.ds(pl.multiple_of(b * WIDE + j * HALF, HALF), HALF)
            grad[HALF:ROWS, there] += fbuf[1, b, :, here].astype(F32) * fsc[1, b, pl.ds(j, 1), :]
            return c

        lax.fori_loop(0, WIDE // HALF, add_far, 0)

    def share(e, buf):
        def go(i, c):
            pltpu.make_async_remote_copy(
                src_ref=buf.at[f], dst_ref=buf.at[f], send_sem=nsend.at[e, i], recv_sem=nrecv.at[e, i],
                device_id=fpeer(i), device_id_type=MESH).start()
            return c

        lax.fori_loop(1, NX * NZ, go, 0)

    def shared(e, buf):
        def go(i, c):
            pltpu.make_async_remote_copy(
                src_ref=buf.at[f], dst_ref=buf.at[(f - i + NX * NZ) % (NX * NZ)],
                send_sem=nsend.at[e, i], recv_sem=nrecv.at[e, i],
                device_id=fpeer(i), device_id_type=MESH).wait_recv()
            return c

        lax.fori_loop(1, NX * NZ, go, 0)
        return jnp.sum(jnp.sum(buf[...], axis=0), keepdims=True)

    def squares(ref):
        def body(i, acc):
            v = ref[pl.ds(pl.multiple_of(i * 8, 8), 8), :]
            return acc + v * v

        acc = lax.fori_loop(0, ROWS // 8, body, jnp.zeros((8, KC), F32))
        total = acc[:, 0:HALF]
        for j in range(1, KC // HALF):
            total += acc[:, j * HALF:(j + 1) * HALF]
        return jnp.sum(total, axis=0, keepdims=True)

    norm[f] = squares(grad)
    share(0, norm)
    transform(grad, xg, 0, 2)
    gather(xg, vg)
    total = shared(0, norm)
    factor = LIMIT / jnp.maximum(jnp.sqrt(total), LIMIT)

    vals[d] = 0.999 * vm[...] + factor * vg[...]

    def v_copy(i, target):
        return pltpu.make_async_remote_copy(
            src_ref=vals.at[d], dst_ref=vals.at[target], send_sem=vsend.at[i], recv_sem=vrecv.at[i],
            device_id=gpeer(i), device_id_type=MESH)

    for i in range(1, GROUPS):
        v_copy(i, d).start()

    xg[...] = mask[...] * (0.999 * xm[...] + factor * xg[...])
    transform(xg, own, 2, 0)
    mom[...] = 0.999 * mom[...] + factor * grad[...] - own[...]
    mom_out = pltpu.make_async_copy(mom, mom_ref.at[0], lsem.at[0])
    mom_out.start()

    for i in range(1, GROUPS):
        v_copy(i, (d - i + GROUPS) % GROUPS).wait_recv()

    def scatter(q, c):
        tall = lax.broadcasted_iota(jnp.int32, (CH, HALF), 0)
        pieces = []
        for g in range(GROUPS):
            hit = tall == (pos_ref[g, pl.ds(q, 1), :] >> 6)
            pieces.append(jnp.where(hit, vals[g, pl.ds(q, 1), :], 0.0))
        h, l = split(jnp.concatenate(pieces, axis=1))
        both = lax.dot_general(jnp.concatenate([h, l], axis=0), cone[q], NT, preferred_element_type=F32)
        quad(xm, q)[...] = (both[0:CH] + both[CH:2 * CH]) * (1.0 / GROUPS)
        return c

    lax.fori_loop(0, 16, scatter, 0)
    spread[f] = squares(xm)
    share(1, spread)
    transform(xm, own, 2, 0)
    upd_out = pltpu.make_async_copy(own, upd_ref, lsem.at[1])
    upd_out.start()
    width = jnp.sqrt(shared(1, spread) / (D * KC) + 1e-6)
    width_ref[...] = jnp.broadcast_to(1.0 / (0.5 * width), (8, HALF))

    def x_sent(s, c):
        for j in range(1, NX):
            a_copy(j, s).wait_send()
        for q in range(2):
            c_copy(q, s).wait_send()
        return c

    def z_sent(s, c):
        for w in range(3):
            for b in range(NB):
                for copy in z_copies(w, b, s):
                    copy.wait_send()
        return c

    def n_sent(i, c):
        for e, buf in enumerate((norm, spread)):
            pltpu.make_async_remote_copy(
                src_ref=buf.at[f], dst_ref=buf.at[f], send_sem=nsend.at[e, i], recv_sem=nrecv.at[e, i],
                device_id=fpeer(i), device_id_type=MESH).wait_send()
        return c

    lax.fori_loop(0, NZ, x_sent, 0)
    lax.fori_loop(0, NZ - 1, z_sent, 0)
    lax.fori_loop(1, NX * NZ, n_sent, 0)
    for j in (1, 3):
        u_copy(j).wait_send()
        u_pass(j).wait_send()
    for b in range(NB):
        for copy in far_copies(b):
            copy.wait_send()
    for i in range(1, GROUPS):
        v_copy(i, d).wait_send()
    mom_out.wait()
    upd_out.wait()


def finish(mom_in, comb_in, width_in, mom_out, upd_out):
    mom_out[...] = mom_in[...]
    upd_out[...] = jnp.tanh(comb_in[...] * width_in[0:1, 0:1])


def local(activations, upstream, momentum, positions):
    dma = pltpu.SemaphoreType.DMA
    hbm = pl.BlockSpec(memory_space=pl.ANY)
    vmem = pl.BlockSpec(memory_space=pltpu.VMEM)
    moved, comb, width = pl.pallas_call(
        kernel,
        out_shape=(
            jax.ShapeDtypeStruct((1, ROWS, KC), F32),
            jax.ShapeDtypeStruct((ROWS, KC), F32),
            jax.ShapeDtypeStruct((8, HALF), F32),
        ),
        in_specs=[hbm] * 5,
        out_specs=(hbm, hbm, vmem),
        scratch_shapes=[
            pltpu.VMEM((GROUPS, 16, HALF), jnp.int32),
            pltpu.VMEM((4, ROWS, ROWS), BF16),
            pltpu.VMEM((GROUPS, 4, 16, 32), jnp.int32),
            pltpu.VMEM((NZ, NX, TOK, HALF), BF16),
            pltpu.VMEM((NZ, 2, 2, TOK, HALF), BF16),
            pltpu.VMEM((NX, TOK, KC), BF16),
            pltpu.VMEM((HALF, NX * TOK), BF16),
            pltpu.VMEM((ROWS, 2 * TOK), BF16),
            pltpu.VMEM((ROWS + HALF, KC), F32),
            pltpu.VMEM((3, NB, NZ - 1, HALF, WIDE), jnp.int16),
            pltpu.VMEM((3, NB, NZ, HALF, WIDE), jnp.int16),
            pltpu.VMEM((3, NB, NZ - 1, 8, HALF), F32),
            pltpu.VMEM((3, NB, NZ, 8, HALF), F32),
            pltpu.VMEM((2, NB, HALF, WIDE), jnp.int16),
            pltpu.VMEM((2, NB, 8, HALF), F32),
            pltpu.VMEM((ROWS, KC), F32),
            pltpu.VMEM((ROWS, KC), F32),
            pltpu.VMEM((ROWS, KC), F32),
            pltpu.VMEM((ROWS, KC), F32),
            pltpu.VMEM((ROWS, KC), F32),
            pltpu.VMEM((ROWS, KC), F32),
            pltpu.VMEM((16, ROWS, GROUPS * HALF), BF16),
            pltpu.VMEM((GROUPS, 16, HALF), F32),
            pltpu.VMEM((16, HALF), F32),
            pltpu.VMEM((16, HALF), F32),
            pltpu.VMEM((NX * NZ, 1, HALF), F32),
            pltpu.VMEM((NX * NZ, 1, HALF), F32),
            dma((NX, NZ)),
            dma((NX, NZ)),
            dma((2, NZ)),
            dma((2, NZ)),
            dma((2, NZ)),
            dma((NX,)),
            dma((NX,)),
            dma((NX,)),
            dma((NX,)),
            dma((3, NB, NZ)),
            dma((3, NB, NZ)),
            dma((3, NB, NZ)),
            dma((3, NB, NZ)),
            dma((2, NB)),
            dma((2, NB)),
            dma((GROUPS,)),
            dma((GROUPS,)),
            dma((2, NX * NZ)),
            dma((2, NX * NZ)),
            dma((3,)),
        ],
        compiler_params=pltpu.CompilerParams(
            collective_id=0, has_side_effects=True, vmem_limit_bytes=56 * 2**20),
        cost_estimate=pl.CostEstimate(flops=7 * 10**9, bytes_accessed=12 * 10**6, transcendentals=0),
    )(activations, upstream, momentum, positions, jnp.asarray(cosine_parts()))
    tile = pl.BlockSpec((STRIP, KC), lambda i: (i, 0))
    deep = pl.BlockSpec((1, STRIP, KC), lambda i: (0, i, 0))
    return pl.pallas_call(
        finish,
        grid=(ROWS // STRIP,),
        out_shape=(
            jax.ShapeDtypeStruct((1, ROWS, KC), F32),
            jax.ShapeDtypeStruct((ROWS, KC), F32),
        ),
        in_specs=[deep, tile, pl.BlockSpec((8, HALF), lambda i: (0, 0))],
        out_specs=(deep, tile),
    )(moved, comb, width)


def solution(mesh):
    placed = (
        P("dp", "fsdp", None),
        P("dp", "fsdp", None),
        P("dp", "fsdp", None),
        P(None, "fsdp", None, None),
    )
    return jax.shard_map(
        local,
        mesh=mesh,
        in_specs=placed,
        out_specs=(P("dp", "fsdp", None), P("fsdp", None)),
        check_vma=False,
    )
```

```python
import math

import jax
import jax.numpy as jnp
import ml_dtypes
import numpy as np
from jax import lax
from jax.experimental import pallas as pl
from jax.experimental.pallas import tpu as pltpu
from jax.sharding import PartitionSpec as P

D = 8192
KC = 1024
CH = 64
TOK = 384
GROUPS = 8
NX = 4
NZ = 8
ROWS = 256
HALF = 128
SPAN = NZ * ROWS
AHEAD_C = 8
AHEAD_A = 8
LAG = 1
NB = 1
STRIP = 128
WIDE = KC // NB
LIMIT = math.sqrt(D * KC)
MESH = pl.DeviceIdType.MESH
F32 = jnp.float32
BF16 = jnp.bfloat16
NT = (((1,), (1,)), ((), ()))
TN = (((0,), (0,)), ((), ()))


def cosine_parts():
    k = np.arange(CH, dtype=np.float64)[:, None]
    n = np.arange(CH, dtype=np.float64)[None, :]
    s = np.where(k == 0, math.sqrt(1.0 / CH), math.sqrt(2.0 / CH))
    c = s * np.cos(math.pi * (2.0 * n + 1.0) * k / (2.0 * CH))
    wide = np.kron(np.eye(4), c)
    high = wide.astype(ml_dtypes.bfloat16)
    low = (wide - high.astype(np.float64)).astype(ml_dtypes.bfloat16)
    return np.stack([high, low, high.T, low.T])


def split(x):
    high = x.astype(BF16)
    return high, (x - high.astype(F32)).astype(BF16)


def dot(a, b):
    return jnp.dot(a, b, preferred_element_type=F32)


def kernel(a_ref, u_ref, m_ref, raw_ref, cos_hbm, mom_ref, upd_ref, width_ref,
           own_pos, pos_t, val_t, own_cone, cos_ref, raw,
           ra, rc, ua, ata, atc, part, sbuf, rbuf, ssc, rsc, fbuf, fsc, grad, xg, xm, mask, mom, own, cone,
           vals, vg, vm, norm, spread, asend, arecv, bsend, brecv, blocal, usend, urecv, psend, precv,
           zsend, zrecv, csend, crecv, fsend, frecv, vsend, vrecv, nsend, nrecv, lsem):
    d = lax.axis_index("dp")
    f = lax.axis_index("fsdp")
    x = f // NZ
    z = f % NZ

    core = d % 2
    way = 1 - 2 * core

    def flip(v, j):
        if j == 1:
            return v + 1 - 2 * (v % 2)
        return (v + 2) % NX if j == 2 else NX - 1 - v

    def pick(v, p):
        return flip(v, 1) + p * (flip(v, 3) - flip(v, 1))

    def at_x(v):
        return {"dp": d, "fsdp": v * NZ + z}

    def xpeer(j):
        return at_x(flip(x, j))

    def zpeer(dz):
        return {"dp": d, "fsdp": x * NZ + (z + dz + NZ) % NZ}

    def gpeer(i):
        return {"dp": (d + i) % GROUPS, "fsdp": f}

    def fpeer(i):
        return {"dp": d, "fsdp": (f + i) % (NX * NZ)}

    barrier = pltpu.get_barrier_semaphore()
    peers = [xpeer(i) for i in range(1, NX)] + [zpeer(-way)]
    peers += [gpeer(i) for i in range(1, GROUPS)]
    for peer in peers:
        pl.semaphore_signal(barrier, inc=1, device_id=peer, device_id_type=MESH)

    def chunk(s):
        return (z - way * (1 + s) + 2 * NZ) % NZ

    def pairing(s):
        return (chunk(s) + core) % 2

    def cols(quarter, s, h):
        start = quarter * SPAN + chunk(s) * ROWS + h * HALF
        return pl.ds(pl.multiple_of(start, HALF), HALF)

    def a_copy(j, s):
        return pltpu.make_async_remote_copy(
            src_ref=a_ref.at[0, :, cols(flip(x, j), s, 0)], dst_ref=ra.at[s, j],
            send_sem=asend.at[j, s], recv_sem=arecv.at[j, s], device_id=xpeer(j), device_id_type=MESH)

    def a_local(s):
        return pltpu.make_async_copy(a_ref.at[0, :, cols(x, s, 0)], ra.at[s, 0], arecv.at[0, s])

    def c_copy(q, s):
        p = pairing(s)
        near = pick(x, p)
        quarter = near if q == 1 else pick(near, 1 - p)
        return pltpu.make_async_remote_copy(
            src_ref=a_ref.at[0, :, cols(quarter, s, 1)], dst_ref=rc.at[s, 1, q],
            send_sem=bsend.at[q, s], recv_sem=brecv.at[q, s], device_id=at_x(near), device_id_type=MESH)

    def c_local(q, s):
        quarter = x if q == 1 else pick(x, 1 - pairing(s))
        return pltpu.make_async_copy(a_ref.at[0, :, cols(quarter, s, 1)], rc.at[s, 0, q], blocal.at[q, s])

    def u_copy(j):
        return pltpu.make_async_remote_copy(
            src_ref=u_ref.at[0], dst_ref=ua.at[j], send_sem=usend.at[j], recv_sem=urecv.at[j],
            device_id=xpeer(j), device_id_type=MESH)

    def u_pass(j):
        rows = pl.ds(0, TOK // 2) if j == 1 else pl.ds(TOK // 2, TOK // 2)
        return pltpu.make_async_remote_copy(
            src_ref=ua.at[4 - j, rows], dst_ref=ua.at[2, rows], send_sem=psend.at[j], recv_sem=precv.at[j],
            device_id=xpeer(j), device_id_type=MESH)

    def pair_of(data, scale, device):
        return [
            pltpu.make_async_remote_copy(
                src_ref=src, dst_ref=dst, send_sem=ss, recv_sem=rs, device_id=device, device_id_type=MESH)
            for src, dst, ss, rs in (data, scale)]

    def z_copies(w, b, s):
        return pair_of(
            (sbuf.at[w, b, s], rbuf.at[w, b, s + 1], zsend.at[w, b, s], zrecv.at[w, b, s + 1]),
            (ssc.at[w, b, s], rsc.at[w, b, s + 1], csend.at[w, b, s], crecv.at[w, b, s + 1]),
            zpeer(way))

    def far_copies(b):
        return pair_of(
            (fbuf.at[0, b], fbuf.at[1, b], fsend.at[0, b], frecv.at[0, b]),
            (fsc.at[0, b], fsc.at[1, b], fsend.at[1, b], frecv.at[1, b]),
            at_x(pick(x, 1 - pairing(NZ - 1))))

    u_local = pltpu.make_async_copy(u_ref.at[0], ua.at[0], urecv.at[0])
    u_local.start()
    m_local = pltpu.make_async_copy(m_ref.at[0], mom, lsem.at[0])
    m_local.start()

    cos_local = pltpu.make_async_copy(cos_hbm, cos_ref, lsem.at[1])
    cos_local.start()
    raw_local = pltpu.make_async_copy(raw_ref, raw, lsem.at[2])
    raw_local.start()

    def start_local(s, c):
        for q in range(2):
            c_local(q, s).start()
        a_local(s).start()
        return c

    lax.fori_loop(0, NZ, start_local, 0)

    pl.semaphore_wait(barrier, len(peers))

    for j in (1, 3):
        u_copy(j).start()

    def start_c(s, c):
        for q in range(2):
            c_copy(q, s).start()
        return c

    def start_a(s, c):
        for j in (1, 3, 2):
            a_copy(j, s).start()
        return c

    lax.fori_loop(0, AHEAD_C, start_c, 0)

    def clear(i, c):
        for w in range(3):
            for b in range(NB):
                rbuf[w, b, 0, pl.ds(pl.multiple_of(i * 16, 16), 16), :] = jnp.zeros((16, WIDE), jnp.int16)
        return c

    lax.fori_loop(0, HALF // 16, clear, 0)
    for w in range(3):
        for b in range(NB):
            rsc[w, b, 0] = jnp.zeros((8, HALF), F32)

    raw_local.wait()
    for a in range(4):
        rows = slice(a * 4, (a + 1) * 4)
        own_pos[rows, :] = jnp.concatenate([raw[d, a, pl.ds(m, 4, stride=4), :] for m in range(4)], axis=1)
        for m in range(4):
            pos_t[m, rows, :] = jnp.concatenate(
                [raw[g, a, pl.ds(m, 4, stride=4), :] for g in range(GROUPS)], axis=1)

    def one_hot_columns(q, c):
        wide = lax.broadcasted_iota(jnp.int32, (ROWS, HALF), 0)
        lane = lax.broadcasted_iota(jnp.int32, (1, HALF), 1)
        col = (own_pos[pl.ds(q, 1), :] & (CH - 1)) + (lane >> 5) * CH
        own_cone[q] = jnp.where(wide == col, 1.0, 0.0).astype(BF16)
        short = lax.broadcasted_iota(jnp.int32, (CH, ROWS), 0)
        for m in range(4):
            hit = short == (pos_t[m, pl.ds(q, 1), :] & (CH - 1))
            cone[q, m * CH:(m + 1) * CH, :] = jnp.where(hit, 1.0, 0.0).astype(BF16)
        return c

    lax.fori_loop(0, 16, one_hot_columns, 0)

    def quad(ref, q):
        rows = pl.ds(pl.multiple_of(q // 4 * CH, CH), CH)
        return ref.at[rows, pl.ds(pl.multiple_of(q % 4 * ROWS, ROWS), ROWS)]

    def own_columns(q):
        return own_cone[q]

    def own_rows(q):
        tall = lax.broadcasted_iota(jnp.int32, (CH, HALF), 0)
        return jnp.where(tall == (own_pos[pl.ds(q, 1), :] >> 6), 1.0, 0.0).astype(BF16)

    def build_mask(q, c):
        quad(mask, q)[...] = lax.dot_general(own_rows(q), own_columns(q), NT, preferred_element_type=F32)
        return c

    lax.fori_loop(0, 16, build_mask, 0)

    def transform(src, dst, left, right):
        def body(j, c):
            at_cols = pl.ds(pl.multiple_of(j * ROWS, ROWS), ROWS)
            h, l = split(src[:, at_cols])
            tall = jnp.concatenate([cos_ref[left], cos_ref[left], cos_ref[left + 1]], axis=1)
            h, l = split(dot(tall, jnp.concatenate([h, l, h], axis=0)))
            deep = jnp.concatenate([cos_ref[right], cos_ref[right], cos_ref[right + 1]], axis=0)
            dst[:, at_cols] = dot(jnp.concatenate([h, l, h], axis=1), deep)
            return c

        lax.fori_loop(0, KC // ROWS, body, 0)

    def gather(src, dst):
        def body(q, c):
            h, l = split(quad(src, q)[...])
            r = own_rows(q)
            t = (lax.dot_general(h, r, TN, preferred_element_type=F32)
                 + lax.dot_general(l, r, TN, preferred_element_type=F32))
            dst[pl.ds(q, 1), :] = jnp.sum(t * own_columns(q).astype(F32), axis=0, keepdims=True)
            return c

        lax.fori_loop(0, 16, body, 0)

    m_local.wait()
    cos_local.wait()
    transform(mom, xm, 0, 2)
    gather(xm, vm)

    u_local.wait()
    for j in (1, 3):
        u_copy(j).wait_recv()
    for j in (1, 3):
        u_pass(j).start()
    lax.fori_loop(0, AHEAD_A, start_a, 0)

    def product_c(s):
        for q in range(2):
            c_local(q, s).wait()
            c_copy(q, s).wait_recv()
        for q in range(2):
            for k in range(2):
                atc[q * HALF:(q + 1) * HALF, k * TOK:(k + 1) * TOK] = rc[s, k, q].T
        near = 1 + 2 * pairing(s)

        def body(j, c):
            here = pl.ds(pl.multiple_of(j * ROWS, ROWS), ROWS)
            both = jnp.concatenate([ua[0, :, here], ua[near, :, here]], axis=0)
            part[0:ROWS, here] = dot(atc[...], both)
            return c

        lax.fori_loop(0, KC // ROWS, body, 0)

    def product_a(s):
        a_local(s).wait()
        for j in range(1, NX):
            a_copy(j, s).wait_recv()
        for j in range(NX):
            ata[:, j * TOK:(j + 1) * TOK] = ra[s, j].T

        def body(j, c):
            here = pl.ds(pl.multiple_of(j * ROWS, ROWS), ROWS)
            part[ROWS:ROWS + HALF, here] = dot(ata[...], ua[:, :, here].reshape(NX * TOK, ROWS))
            return c

        lax.fori_loop(0, KC // ROWS, body, 0)

    def encode(v, codes, scales, j, here):
        top = jnp.maximum(jnp.max(jnp.abs(v), axis=0, keepdims=True), 1e-30)
        scales[pl.ds(j, 1), :] = top * (1.0 / 32767.0)
        code = lax.round(v * (32767.0 / top), lax.RoundingMethod.TO_NEAREST_EVEN)
        codes[:, here] = code.astype(jnp.int32).astype(jnp.int16)

    def reduce_step(w, s, last):
        for b in range(NB):
            @pl.when(s > 0)
            def _():
                for copy in z_copies(w, b, s - 1):
                    copy.wait_recv()

            def body(j, c):
                here = pl.ds(pl.multiple_of(j * HALF, HALF), HALF)
                there = pl.ds(pl.multiple_of(b * WIDE + j * HALF, HALF), HALF)
                v = part[w * HALF:(w + 1) * HALF, there]
                v += rbuf[w, b, s, :, here].astype(F32) * rsc[w, b, s, pl.ds(j, 1), :]
                if not last:
                    encode(v, sbuf.at[w, b, s], ssc.at[w, b, s], j, here)
                elif w == 0:
                    encode(v, fbuf.at[0, b], fsc.at[0, b], j, here)
                else:
                    top = HALF * (w % 2)
                    grad[top:top + HALF, there] = v
                return c

            lax.fori_loop(0, WIDE // HALF, body, 0)
            if not last:
                for copy in z_copies(w, b, s):
                    copy.start()
            elif w == 0:
                for copy in far_copies(b):
                    copy.start()

    def step_c(s, last):
        @pl.when(s + AHEAD_C < NZ)
        def _():
            start_c(s + AHEAD_C, 0)
        product_c(s)
        reduce_step(0, s, last)
        reduce_step(1, s, last)

    def step_a(s, last):
        @pl.when(s + AHEAD_A < NZ)
        def _():
            start_a(s + AHEAD_A, 0)
        product_a(s)
        reduce_step(2, s, last)

    def only_c(t, c):
        step_c(t, False)
        return c

    def mixed(t, c):
        step_c(t, False)
        step_a(t - LAG, False)
        return c

    def only_a(t, c):
        step_a(t - LAG, False)
        return c

    lax.fori_loop(0, LAG, only_c, 0)
    for j in (1, 3):
        u_pass(j).wait_recv()
    lax.fori_loop(LAG, NZ - 1, mixed, 0)
    step_c(NZ - 1, True)
    lax.fori_loop(NZ - 1, NZ - 1 + LAG, only_a, 0)
    step_a(NZ - 1, True)

    for b in range(NB):
        for copy in far_copies(b):
            copy.wait_recv()

        def add_far(j, c):
            here = pl.ds(pl.multiple_of(j * HALF, HALF), HALF)
            there = pl.ds(pl.multiple_of(b * WIDE + j * HALF, HALF), HALF)
            grad[HALF:ROWS, there] += fbuf[1, b, :, here].astype(F32) * fsc[1, b, pl.ds(j, 1), :]
            return c

        lax.fori_loop(0, WIDE // HALF, add_far, 0)

    def spread_copy(e, buf, i):
        return pltpu.make_async_remote_copy(
            src_ref=buf.at[f], dst_ref=buf.at[f], send_sem=nsend.at[e], recv_sem=nrecv.at[e],
            device_id=fpeer(i), device_id_type=MESH)

    def all_copies(e, buf):
        others = buf.at[pl.ds(0, NX * NZ - 1)]
        return pltpu.make_async_remote_copy(
            src_ref=others, dst_ref=others, send_sem=nsend.at[e], recv_sem=nrecv.at[e],
            device_id=fpeer(1), device_id_type=MESH)

    def share(e, buf):
        def go(i, c):
            spread_copy(e, buf, i).start()
            return c

        lax.fori_loop(1, NX * NZ, go, 0)

    def shared(e, buf):
        all_copies(e, buf).wait_recv()
        return jnp.sum(jnp.sum(buf[...], axis=0), keepdims=True)

    def squares(ref):
        def body(i, acc):
            v = ref[pl.ds(pl.multiple_of(i * 8, 8), 8), :]
            return acc + v * v

        acc = lax.fori_loop(0, ROWS // 8, body, jnp.zeros((8, KC), F32))
        total = acc[:, 0:HALF]
        for j in range(1, KC // HALF):
            total += acc[:, j * HALF:(j + 1) * HALF]
        return jnp.sum(total, axis=0, keepdims=True)

    norm[f] = squares(grad)
    share(0, norm)
    transform(grad, xg, 0, 2)
    gather(xg, vg)

    def x_sent(s, c):
        for j in range(1, NX):
            a_copy(j, s).wait_send()
        for q in range(2):
            c_copy(q, s).wait_send()
        return c

    def z_sent(s, c):
        for w in range(3):
            for b in range(NB):
                for copy in z_copies(w, b, s):
                    copy.wait_send()
        return c

    lax.fori_loop(0, NZ, x_sent, 0)
    lax.fori_loop(0, NZ - 1, z_sent, 0)
    for j in (1, 3):
        u_copy(j).wait_send()
        u_pass(j).wait_send()
    for b in range(NB):
        for copy in far_copies(b):
            copy.wait_send()
    all_copies(0, norm).wait_send()
    total = shared(0, norm)
    factor = LIMIT / jnp.maximum(jnp.sqrt(total), LIMIT)

    vals[d] = 0.999 * vm[...] + factor * vg[...]

    def v_copy(i, target):
        return pltpu.make_async_remote_copy(
            src_ref=vals.at[d], dst_ref=vals.at[target], send_sem=vsend.at[i], recv_sem=vrecv.at[i],
            device_id=gpeer(i), device_id_type=MESH)

    for i in range(1, GROUPS):
        v_copy(i, d).start()

    xg[...] = mask[...] * (0.999 * xm[...] + factor * xg[...])
    transform(xg, own, 2, 0)
    mom[...] = 0.999 * mom[...] + factor * grad[...] - own[...]
    mom_out = pltpu.make_async_copy(mom, mom_ref.at[0], lsem.at[0])
    mom_out.start()

    for i in range(1, GROUPS):
        v_copy(i, (d - i + GROUPS) % GROUPS).wait_recv()

    for m in range(4):
        val_t[m] = jnp.concatenate([vals[g, :, m * 32:(m + 1) * 32] for g in range(GROUPS)], axis=1)

    def scatter(q, c):
        tall = lax.broadcasted_iota(jnp.int32, (CH, ROWS), 0)
        pieces = []
        for m in range(4):
            hit = tall == (pos_t[m, pl.ds(q, 1), :] >> 6)
            pieces += split(jnp.where(hit, val_t[m, pl.ds(q, 1), :], 0.0))
        every = lax.dot_general(jnp.concatenate(pieces, axis=0), cone[q], NT, preferred_element_type=F32)
        block = lax.broadcasted_iota(jnp.int32, (CH, ROWS), 1) >> 6
        total = jnp.zeros((CH, ROWS), F32)
        for m in range(4):
            both = every[m * HALF:m * HALF + CH] + every[m * HALF + CH:(m + 1) * HALF]
            total = jnp.where(block == m, both, total)
        quad(xm, q)[...] = total * (1.0 / GROUPS)
        return c

    lax.fori_loop(0, 16, scatter, 0)
    spread[f] = squares(xm)
    share(1, spread)
    transform(xm, own, 2, 0)
    upd_out = pltpu.make_async_copy(own, upd_ref, lsem.at[1])
    upd_out.start()
    width = jnp.sqrt(shared(1, spread) / (D * KC) + 1e-6)
    width_ref[...] = jnp.broadcast_to(1.0 / (0.5 * width), (8, HALF))

    all_copies(1, spread).wait_send()
    for i in range(1, GROUPS):
        v_copy(i, d).wait_send()
    mom_out.wait()
    upd_out.wait()


def finish(mom_in, comb_in, width_in, mom_out, upd_out):
    mom_out[...] = mom_in[...]
    upd_out[...] = jnp.tanh(comb_in[...] * width_in[0:1, 0:1])


def local(activations, upstream, momentum, positions):
    dma = pltpu.SemaphoreType.DMA
    hbm = pl.BlockSpec(memory_space=pl.ANY)
    vmem = pl.BlockSpec(memory_space=pltpu.VMEM)
    moved, comb, width = pl.pallas_call(
        kernel,
        out_shape=(
            jax.ShapeDtypeStruct((1, ROWS, KC), F32),
            jax.ShapeDtypeStruct((ROWS, KC), F32),
            jax.ShapeDtypeStruct((8, HALF), F32),
        ),
        in_specs=[hbm] * 5,
        out_specs=(hbm, hbm, vmem),
        scratch_shapes=[
            pltpu.VMEM((16, HALF), jnp.int32),
            pltpu.VMEM((4, 16, ROWS), jnp.int32),
            pltpu.VMEM((4, 16, ROWS), F32),
            pltpu.VMEM((16, ROWS, HALF), BF16),
            pltpu.VMEM((4, ROWS, ROWS), BF16),
            pltpu.VMEM((GROUPS, 4, 16, 32), jnp.int32),
            pltpu.VMEM((NZ, NX, TOK, HALF), BF16),
            pltpu.VMEM((NZ, 2, 2, TOK, HALF), BF16),
            pltpu.VMEM((NX, TOK, KC), BF16),
            pltpu.VMEM((HALF, NX * TOK), BF16),
            pltpu.VMEM((ROWS, 2 * TOK), BF16),
            pltpu.VMEM((ROWS + HALF, KC), F32),
            pltpu.VMEM((3, NB, NZ - 1, HALF, WIDE), jnp.int16),
            pltpu.VMEM((3, NB, NZ, HALF, WIDE), jnp.int16),
            pltpu.VMEM((3, NB, NZ - 1, 8, HALF), F32),
            pltpu.VMEM((3, NB, NZ, 8, HALF), F32),
            pltpu.VMEM((2, NB, HALF, WIDE), jnp.int16),
            pltpu.VMEM((2, NB, 8, HALF), F32),
            pltpu.VMEM((ROWS, KC), F32),
            pltpu.VMEM((ROWS, KC), F32),
            pltpu.VMEM((ROWS, KC), F32),
            pltpu.VMEM((ROWS, KC), F32),
            pltpu.VMEM((ROWS, KC), F32),
            pltpu.VMEM((ROWS, KC), F32),
            pltpu.VMEM((16, ROWS, ROWS), BF16),
            pltpu.VMEM((GROUPS, 16, HALF), F32),
            pltpu.VMEM((16, HALF), F32),
            pltpu.VMEM((16, HALF), F32),
            pltpu.VMEM((NX * NZ, 1, HALF), F32),
            pltpu.VMEM((NX * NZ, 1, HALF), F32),
            dma((NX, NZ)),
            dma((NX, NZ)),
            dma((2, NZ)),
            dma((2, NZ)),
            dma((2, NZ)),
            dma((NX,)),
            dma((NX,)),
            dma((NX,)),
            dma((NX,)),
            dma((3, NB, NZ)),
            dma((3, NB, NZ)),
            dma((3, NB, NZ)),
            dma((3, NB, NZ)),
            dma((2, NB)),
            dma((2, NB)),
            dma((GROUPS,)),
            dma((GROUPS,)),
            dma((2,)),
            dma((2,)),
            dma((3,)),
        ],
        compiler_params=pltpu.CompilerParams(
            collective_id=0, has_side_effects=True, vmem_limit_bytes=56 * 2**20),
        cost_estimate=pl.CostEstimate(flops=7 * 10**9, bytes_accessed=12 * 10**6, transcendentals=0),
    )(activations, upstream, momentum, positions, jnp.asarray(cosine_parts()))
    tile = pl.BlockSpec((STRIP, KC), lambda i: (i, 0))
    deep = pl.BlockSpec((1, STRIP, KC), lambda i: (0, i, 0))
    return pl.pallas_call(
        finish,
        grid=(ROWS // STRIP,),
        out_shape=(
            jax.ShapeDtypeStruct((1, ROWS, KC), F32),
            jax.ShapeDtypeStruct((ROWS, KC), F32),
        ),
        in_specs=[deep, tile, pl.BlockSpec((8, HALF), lambda i: (0, 0))],
        out_specs=(deep, tile),
    )(moved, comb, width)


def solution(mesh):
    placed = (
        P("dp", "fsdp", None),
        P("dp", "fsdp", None),
        P("dp", "fsdp", None),
        P(None, "fsdp", None, None),
    )
    return jax.shard_map(
        local,
        mesh=mesh,
        in_specs=placed,
        out_specs=(P("dp", "fsdp", None), P("fsdp", None)),
        check_vma=False,
    )
```

```python
import math

import jax
import jax.numpy as jnp
import ml_dtypes
import numpy as np
from jax import lax
from jax.experimental import pallas as pl
from jax.experimental.pallas import tpu as pltpu
from jax.sharding import PartitionSpec as P

D = 8192
KC = 1024
CH = 64
TOK = 384
GROUPS = 8
NX = 4
NZ = 8
ROWS = 256
HALF = 128
SPAN = NZ * ROWS
FIRST_C = 2
AHEAD_C = 4
AHEAD_A = 3
LAG = 1
NB = 1
STRIP = 128
WIDE = KC // NB
LIMIT = math.sqrt(D * KC)
MESH = pl.DeviceIdType.MESH
F32 = jnp.float32
BF16 = jnp.bfloat16
NT = (((1,), (1,)), ((), ()))
TN = (((0,), (0,)), ((), ()))


def cosine_parts():
    k = np.arange(CH, dtype=np.float64)[:, None]
    n = np.arange(CH, dtype=np.float64)[None, :]
    s = np.where(k == 0, math.sqrt(1.0 / CH), math.sqrt(2.0 / CH))
    c = s * np.cos(math.pi * (2.0 * n + 1.0) * k / (2.0 * CH))
    wide = np.kron(np.eye(4), c)
    high = wide.astype(ml_dtypes.bfloat16)
    low = (wide - high.astype(np.float64)).astype(ml_dtypes.bfloat16)
    return np.stack([high, low, high.T, low.T])


def split(x):
    high = x.astype(BF16)
    return high, (x - high.astype(F32)).astype(BF16)


def dot(a, b):
    return jnp.dot(a, b, preferred_element_type=F32)


def kernel(a_ref, u_ref, m_ref, raw_ref, cos_hbm, mom_ref, upd_ref, width_ref,
           own_pos, pos_t, val_t, own_cone, cos_ref, raw,
           ra, rc, ua, ata, atc, part, sbuf, rbuf, ssc, rsc, fbuf, fsc, grad, xg, xm, mask, mom, own, cone,
           vals, vg, vm, norm, spread, asend, arecv, bsend, brecv, blocal, usend, urecv, psend, precv,
           zsend, zrecv, csend, crecv, fsend, frecv, vsend, vrecv, nsend, nrecv, lsem):
    d = lax.axis_index("dp")
    f = lax.axis_index("fsdp")
    x = f // NZ
    z = f % NZ

    core = d % 2
    way = 1 - 2 * core

    def flip(v, j):
        if j == 1:
            return v + 1 - 2 * (v % 2)
        return (v + 2) % NX if j == 2 else NX - 1 - v

    def pick(v, p):
        return flip(v, 1) + p * (flip(v, 3) - flip(v, 1))

    def at_x(v):
        return {"dp": d, "fsdp": v * NZ + z}

    def xpeer(j):
        return at_x(flip(x, j))

    def zpeer(dz):
        return {"dp": d, "fsdp": x * NZ + (z + dz + NZ) % NZ}

    def gpeer(i):
        return {"dp": (d + i) % GROUPS, "fsdp": f}

    def fpeer(i):
        return {"dp": d, "fsdp": (f + i) % (NX * NZ)}

    barrier = pltpu.get_barrier_semaphore()
    peers = [xpeer(i) for i in range(1, NX)] + [zpeer(-way)]
    peers += [gpeer(i) for i in range(1, GROUPS)]
    for peer in peers:
        pl.semaphore_signal(barrier, inc=1, device_id=peer, device_id_type=MESH)

    def chunk(s):
        return (z - way * (1 + s) + 2 * NZ) % NZ

    def pairing(s):
        return (chunk(s) + core) % 2

    def cols(quarter, s, h):
        start = quarter * SPAN + chunk(s) * ROWS + h * HALF
        return pl.ds(pl.multiple_of(start, HALF), HALF)

    def a_copy(j, s):
        return pltpu.make_async_remote_copy(
            src_ref=a_ref.at[0, :, cols(flip(x, j), s, 0)], dst_ref=ra.at[s, j],
            send_sem=asend.at[j, s], recv_sem=arecv.at[j, s], device_id=xpeer(j), device_id_type=MESH)

    def a_local(s):
        return pltpu.make_async_copy(a_ref.at[0, :, cols(x, s, 0)], ra.at[s, 0], arecv.at[0, s])

    def c_copy(q, s):
        p = pairing(s)
        near = pick(x, p)
        quarter = near if q == 1 else pick(near, 1 - p)
        return pltpu.make_async_remote_copy(
            src_ref=a_ref.at[0, :, cols(quarter, s, 1)], dst_ref=rc.at[s, 1, q],
            send_sem=bsend.at[q, s], recv_sem=brecv.at[q, s], device_id=at_x(near), device_id_type=MESH)

    def c_local(q, s):
        quarter = x if q == 1 else pick(x, 1 - pairing(s))
        return pltpu.make_async_copy(a_ref.at[0, :, cols(quarter, s, 1)], rc.at[s, 0, q], blocal.at[q, s])

    def u_copy(j):
        return pltpu.make_async_remote_copy(
            src_ref=u_ref.at[0], dst_ref=ua.at[j], send_sem=usend.at[j], recv_sem=urecv.at[j],
            device_id=xpeer(j), device_id_type=MESH)

    def u_pass(j):
        rows = pl.ds(0, TOK // 2) if j == 1 else pl.ds(TOK // 2, TOK // 2)
        return pltpu.make_async_remote_copy(
            src_ref=ua.at[4 - j, rows], dst_ref=ua.at[2, rows], send_sem=psend.at[j], recv_sem=precv.at[j],
            device_id=xpeer(j), device_id_type=MESH)

    def pair_of(data, scale, device):
        return [
            pltpu.make_async_remote_copy(
                src_ref=src, dst_ref=dst, send_sem=ss, recv_sem=rs, device_id=device, device_id_type=MESH)
            for src, dst, ss, rs in (data, scale)]

    def z_copies(w, b, s):
        return pair_of(
            (sbuf.at[w, b, s], rbuf.at[w, b, s + 1], zsend.at[w, b, s], zrecv.at[w, b, s + 1]),
            (ssc.at[w, b, s], rsc.at[w, b, s + 1], csend.at[w, b, s], crecv.at[w, b, s + 1]),
            zpeer(way))

    def far_copies(b):
        return pair_of(
            (fbuf.at[0, b], fbuf.at[1, b], fsend.at[0, b], frecv.at[0, b]),
            (fsc.at[0, b], fsc.at[1, b], fsend.at[1, b], frecv.at[1, b]),
            at_x(pick(x, 1 - pairing(NZ - 1))))

    u_local = pltpu.make_async_copy(u_ref.at[0], ua.at[0], urecv.at[0])
    u_local.start()
    m_local = pltpu.make_async_copy(m_ref.at[0], mom, lsem.at[0])
    m_local.start()

    cos_local = pltpu.make_async_copy(cos_hbm, cos_ref, lsem.at[1])
    cos_local.start()
    raw_local = pltpu.make_async_copy(raw_ref, raw, lsem.at[2])
    raw_local.start()

    def start_local(s, c):
        for q in range(2):
            c_local(q, s).start()
        a_local(s).start()
        return c

    lax.fori_loop(0, NZ, start_local, 0)

    pl.semaphore_wait(barrier, len(peers))

    for j in (1, 3):
        u_copy(j).start()

    def start_c(s, c):
        for q in range(2):
            c_copy(q, s).start()
        return c

    def start_a(s, c):
        for j in (1, 3, 2):
            a_copy(j, s).start()
        return c

    lax.fori_loop(0, FIRST_C, start_c, 0)

    def clear(i, c):
        for w in range(3):
            for b in range(NB):
                rbuf[w, b, 0, pl.ds(pl.multiple_of(i * 16, 16), 16), :] = jnp.zeros((16, WIDE), jnp.int16)
        return c

    lax.fori_loop(0, HALF // 16, clear, 0)
    for w in range(3):
        for b in range(NB):
            rsc[w, b, 0] = jnp.zeros((8, HALF), F32)

    raw_local.wait()
    for a in range(4):
        rows = slice(a * 4, (a + 1) * 4)
        own_pos[rows, :] = jnp.concatenate([raw[d, a, pl.ds(m, 4, stride=4), :] for m in range(4)], axis=1)
        for m in range(4):
            pos_t[m, rows, :] = jnp.concatenate(
                [raw[g, a, pl.ds(m, 4, stride=4), :] for g in range(GROUPS)], axis=1)

    def one_hot_columns(q, c):
        wide = lax.broadcasted_iota(jnp.int32, (ROWS, HALF), 0)
        lane = lax.broadcasted_iota(jnp.int32, (1, HALF), 1)
        col = (own_pos[pl.ds(q, 1), :] & (CH - 1)) + (lane >> 5) * CH
        own_cone[q] = jnp.where(wide == col, 1.0, 0.0).astype(BF16)
        short = lax.broadcasted_iota(jnp.int32, (CH, ROWS), 0)
        for m in range(4):
            hit = short == (pos_t[m, pl.ds(q, 1), :] & (CH - 1))
            cone[q, m * CH:(m + 1) * CH, :] = jnp.where(hit, 1.0, 0.0).astype(BF16)
        return c

    lax.fori_loop(0, 16, one_hot_columns, 0)

    def quad(ref, q):
        rows = pl.ds(pl.multiple_of(q // 4 * CH, CH), CH)
        return ref.at[rows, pl.ds(pl.multiple_of(q % 4 * ROWS, ROWS), ROWS)]

    def own_columns(q):
        return own_cone[q]

    def own_rows(q):
        tall = lax.broadcasted_iota(jnp.int32, (CH, HALF), 0)
        return jnp.where(tall == (own_pos[pl.ds(q, 1), :] >> 6), 1.0, 0.0).astype(BF16)

    def build_mask(q, c):
        quad(mask, q)[...] = lax.dot_general(own_rows(q), own_columns(q), NT, preferred_element_type=F32)
        return c

    lax.fori_loop(0, 16, build_mask, 0)

    def transform(src, dst, left, right):
        def body(j, c):
            at_cols = pl.ds(pl.multiple_of(j * ROWS, ROWS), ROWS)
            h, l = split(src[:, at_cols])
            tall = jnp.concatenate([cos_ref[left], cos_ref[left], cos_ref[left + 1]], axis=1)
            h, l = split(dot(tall, jnp.concatenate([h, l, h], axis=0)))
            deep = jnp.concatenate([cos_ref[right], cos_ref[right], cos_ref[right + 1]], axis=0)
            dst[:, at_cols] = dot(jnp.concatenate([h, l, h], axis=1), deep)
            return c

        lax.fori_loop(0, KC // ROWS, body, 0)

    def gather(src, dst):
        def body(q, c):
            h, l = split(quad(src, q)[...])
            r = own_rows(q)
            t = (lax.dot_general(h, r, TN, preferred_element_type=F32)
                 + lax.dot_general(l, r, TN, preferred_element_type=F32))
            dst[pl.ds(q, 1), :] = jnp.sum(t * own_columns(q).astype(F32), axis=0, keepdims=True)
            return c

        lax.fori_loop(0, 16, body, 0)

    m_local.wait()
    cos_local.wait()
    transform(mom, xm, 0, 2)
    gather(xm, vm)

    u_local.wait()
    for j in (1, 3):
        u_copy(j).wait_recv()
    for j in (1, 3):
        u_pass(j).start()
    lax.fori_loop(FIRST_C, AHEAD_C, start_c, 0)
    lax.fori_loop(0, AHEAD_A, start_a, 0)

    def product_c(s):
        for q in range(2):
            c_local(q, s).wait()
            c_copy(q, s).wait_recv()
        for q in range(2):
            for k in range(2):
                atc[q * HALF:(q + 1) * HALF, k * TOK:(k + 1) * TOK] = rc[s, k, q].T
        near = 1 + 2 * pairing(s)

        def body(j, c):
            here = pl.ds(pl.multiple_of(j * ROWS, ROWS), ROWS)
            both = jnp.concatenate([ua[0, :, here], ua[near, :, here]], axis=0)
            part[0:ROWS, here] = dot(atc[...], both)
            return c

        lax.fori_loop(0, KC // ROWS, body, 0)

    def product_a(s):
        a_local(s).wait()
        for j in range(1, NX):
            a_copy(j, s).wait_recv()
        for j in range(NX):
            ata[:, j * TOK:(j + 1) * TOK] = ra[s, j].T

        def body(j, c):
            here = pl.ds(pl.multiple_of(j * ROWS, ROWS), ROWS)
            part[ROWS:ROWS + HALF, here] = dot(ata[...], ua[:, :, here].reshape(NX * TOK, ROWS))
            return c

        lax.fori_loop(0, KC // ROWS, body, 0)

    def encode(v, codes, scales, j, here):
        top = jnp.maximum(jnp.max(jnp.abs(v), axis=0, keepdims=True), 1e-30)
        scales[pl.ds(j, 1), :] = top * (1.0 / 32767.0)
        code = lax.round(v * (32767.0 / top), lax.RoundingMethod.TO_NEAREST_EVEN)
        codes[:, here] = code.astype(jnp.int32).astype(jnp.int16)

    def reduce_step(w, s, last):
        for b in range(NB):
            @pl.when(s > 0)
            def _():
                for copy in z_copies(w, b, s - 1):
                    copy.wait_recv()

            def body(j, c):
                here = pl.ds(pl.multiple_of(j * HALF, HALF), HALF)
                there = pl.ds(pl.multiple_of(b * WIDE + j * HALF, HALF), HALF)
                v = part[w * HALF:(w + 1) * HALF, there]
                v += rbuf[w, b, s, :, here].astype(F32) * rsc[w, b, s, pl.ds(j, 1), :]
                if not last:
                    encode(v, sbuf.at[w, b, s], ssc.at[w, b, s], j, here)
                elif w == 0:
                    encode(v, fbuf.at[0, b], fsc.at[0, b], j, here)
                else:
                    top = HALF * (w % 2)
                    grad[top:top + HALF, there] = v
                return c

            lax.fori_loop(0, WIDE // HALF, body, 0)
            if not last:
                for copy in z_copies(w, b, s):
                    copy.start()
            elif w == 0:
                for copy in far_copies(b):
                    copy.start()

    def step_c(s, last):
        @pl.when(s + AHEAD_C < NZ)
        def _():
            start_c(s + AHEAD_C, 0)
        product_c(s)
        reduce_step(0, s, last)
        reduce_step(1, s, last)

    def step_a(s, last):
        @pl.when(s + AHEAD_A < NZ)
        def _():
            start_a(s + AHEAD_A, 0)
        product_a(s)
        reduce_step(2, s, last)

    def only_c(t, c):
        step_c(t, False)
        return c

    def mixed(t, c):
        step_c(t, False)
        step_a(t - LAG, False)
        return c

    def only_a(t, c):
        step_a(t - LAG, False)
        return c

    lax.fori_loop(0, LAG, only_c, 0)
    for j in (1, 3):
        u_pass(j).wait_recv()
    lax.fori_loop(LAG, NZ - 1, mixed, 0)
    step_c(NZ - 1, True)
    lax.fori_loop(NZ - 1, NZ - 1 + LAG, only_a, 0)
    step_a(NZ - 1, True)

    for b in range(NB):
        for copy in far_copies(b):
            copy.wait_recv()

        def add_far(j, c):
            here = pl.ds(pl.multiple_of(j * HALF, HALF), HALF)
            there = pl.ds(pl.multiple_of(b * WIDE + j * HALF, HALF), HALF)
            grad[HALF:ROWS, there] += fbuf[1, b, :, here].astype(F32) * fsc[1, b, pl.ds(j, 1), :]
            return c

        lax.fori_loop(0, WIDE // HALF, add_far, 0)

    def spread_copy(e, buf, i):
        return pltpu.make_async_remote_copy(
            src_ref=buf.at[f], dst_ref=buf.at[f], send_sem=nsend.at[e], recv_sem=nrecv.at[e],
            device_id=fpeer(i), device_id_type=MESH)

    def all_copies(e, buf):
        others = buf.at[pl.ds(0, NX * NZ - 1)]
        return pltpu.make_async_remote_copy(
            src_ref=others, dst_ref=others, send_sem=nsend.at[e], recv_sem=nrecv.at[e],
            device_id=fpeer(1), device_id_type=MESH)

    def share(e, buf):
        def go(i, c):
            spread_copy(e, buf, i).start()
            return c

        lax.fori_loop(1, NX * NZ, go, 0)

    def shared(e, buf):
        all_copies(e, buf).wait_recv()
        return jnp.sum(jnp.sum(buf[...], axis=0), keepdims=True)

    def squares(ref):
        def body(i, acc):
            v = ref[pl.ds(pl.multiple_of(i * 8, 8), 8), :]
            return acc + v * v

        acc = lax.fori_loop(0, ROWS // 8, body, jnp.zeros((8, KC), F32))
        total = acc[:, 0:HALF]
        for j in range(1, KC // HALF):
            total += acc[:, j * HALF:(j + 1) * HALF]
        return jnp.sum(total, axis=0, keepdims=True)

    norm[f] = squares(grad)
    share(0, norm)
    transform(grad, xg, 0, 2)
    gather(xg, vg)

    def x_sent(s, c):
        for j in range(1, NX):
            a_copy(j, s).wait_send()
        for q in range(2):
            c_copy(q, s).wait_send()
        return c

    def z_sent(s, c):
        for w in range(3):
            for b in range(NB):
                for copy in z_copies(w, b, s):
                    copy.wait_send()
        return c

    lax.fori_loop(0, NZ, x_sent, 0)
    lax.fori_loop(0, NZ - 1, z_sent, 0)
    for j in (1, 3):
        u_copy(j).wait_send()
        u_pass(j).wait_send()
    for b in range(NB):
        for copy in far_copies(b):
            copy.wait_send()
    all_copies(0, norm).wait_send()
    total = shared(0, norm)
    factor = LIMIT / jnp.maximum(jnp.sqrt(total), LIMIT)

    vals[d] = 0.999 * vm[...] + factor * vg[...]

    def v_copy(i, target):
        return pltpu.make_async_remote_copy(
            src_ref=vals.at[d], dst_ref=vals.at[target], send_sem=vsend.at[i], recv_sem=vrecv.at[i],
            device_id=gpeer(i), device_id_type=MESH)

    for i in range(1, GROUPS):
        v_copy(i, d).start()

    xg[...] = mask[...] * (0.999 * xm[...] + factor * xg[...])
    transform(xg, own, 2, 0)
    mom[...] = 0.999 * mom[...] + factor * grad[...] - own[...]
    mom_out = pltpu.make_async_copy(mom, mom_ref.at[0], lsem.at[0])
    mom_out.start()

    for i in range(1, GROUPS):
        v_copy(i, (d - i + GROUPS) % GROUPS).wait_recv()

    for m in range(4):
        val_t[m] = jnp.concatenate([vals[g, :, m * 32:(m + 1) * 32] for g in range(GROUPS)], axis=1)

    def scatter(q, c):
        tall = lax.broadcasted_iota(jnp.int32, (CH, ROWS), 0)
        pieces = []
        for m in range(4):
            hit = tall == (pos_t[m, pl.ds(q, 1), :] >> 6)
            pieces += split(jnp.where(hit, val_t[m, pl.ds(q, 1), :], 0.0))
        every = lax.dot_general(jnp.concatenate(pieces, axis=0), cone[q], NT, preferred_element_type=F32)
        block = lax.broadcasted_iota(jnp.int32, (CH, ROWS), 1) >> 6
        total = jnp.zeros((CH, ROWS), F32)
        for m in range(4):
            both = every[m * HALF:m * HALF + CH] + every[m * HALF + CH:(m + 1) * HALF]
            total = jnp.where(block == m, both, total)
        quad(xm, q)[...] = total * (1.0 / GROUPS)
        return c

    lax.fori_loop(0, 16, scatter, 0)
    spread[f] = squares(xm)
    share(1, spread)
    transform(xm, own, 2, 0)
    upd_out = pltpu.make_async_copy(own, upd_ref, lsem.at[1])
    upd_out.start()
    width = jnp.sqrt(shared(1, spread) / (D * KC) + 1e-6)
    width_ref[...] = jnp.broadcast_to(1.0 / (0.5 * width), (8, HALF))

    all_copies(1, spread).wait_send()
    for i in range(1, GROUPS):
        v_copy(i, d).wait_send()
    mom_out.wait()
    upd_out.wait()


def finish(mom_in, comb_in, width_in, mom_out, upd_out):
    mom_out[...] = mom_in[...]
    upd_out[...] = jnp.tanh(comb_in[...] * width_in[0:1, 0:1])


def local(activations, upstream, momentum, positions):
    dma = pltpu.SemaphoreType.DMA
    hbm = pl.BlockSpec(memory_space=pl.ANY)
    vmem = pl.BlockSpec(memory_space=pltpu.VMEM)
    moved, comb, width = pl.pallas_call(
        kernel,
        out_shape=(
            jax.ShapeDtypeStruct((1, ROWS, KC), F32),
            jax.ShapeDtypeStruct((ROWS, KC), F32),
            jax.ShapeDtypeStruct((8, HALF), F32),
        ),
        in_specs=[hbm] * 5,
        out_specs=(hbm, hbm, vmem),
        scratch_shapes=[
            pltpu.VMEM((16, HALF), jnp.int32),
            pltpu.VMEM((4, 16, ROWS), jnp.int32),
            pltpu.VMEM((4, 16, ROWS), F32),
            pltpu.VMEM((16, ROWS, HALF), BF16),
            pltpu.VMEM((4, ROWS, ROWS), BF16),
            pltpu.VMEM((GROUPS, 4, 16, 32), jnp.int32),
            pltpu.VMEM((NZ, NX, TOK, HALF), BF16),
            pltpu.VMEM((NZ, 2, 2, TOK, HALF), BF16),
            pltpu.VMEM((NX, TOK, KC), BF16),
            pltpu.VMEM((HALF, NX * TOK), BF16),
            pltpu.VMEM((ROWS, 2 * TOK), BF16),
            pltpu.VMEM((ROWS + HALF, KC), F32),
            pltpu.VMEM((3, NB, NZ - 1, HALF, WIDE), jnp.int16),
            pltpu.VMEM((3, NB, NZ, HALF, WIDE), jnp.int16),
            pltpu.VMEM((3, NB, NZ - 1, 8, HALF), F32),
            pltpu.VMEM((3, NB, NZ, 8, HALF), F32),
            pltpu.VMEM((2, NB, HALF, WIDE), jnp.int16),
            pltpu.VMEM((2, NB, 8, HALF), F32),
            pltpu.VMEM((ROWS, KC), F32),
            pltpu.VMEM((ROWS, KC), F32),
            pltpu.VMEM((ROWS, KC), F32),
            pltpu.VMEM((ROWS, KC), F32),
            pltpu.VMEM((ROWS, KC), F32),
            pltpu.VMEM((ROWS, KC), F32),
            pltpu.VMEM((16, ROWS, ROWS), BF16),
            pltpu.VMEM((GROUPS, 16, HALF), F32),
            pltpu.VMEM((16, HALF), F32),
            pltpu.VMEM((16, HALF), F32),
            pltpu.VMEM((NX * NZ, 1, HALF), F32),
            pltpu.VMEM((NX * NZ, 1, HALF), F32),
            dma((NX, NZ)),
            dma((NX, NZ)),
            dma((2, NZ)),
            dma((2, NZ)),
            dma((2, NZ)),
            dma((NX,)),
            dma((NX,)),
            dma((NX,)),
            dma((NX,)),
            dma((3, NB, NZ)),
            dma((3, NB, NZ)),
            dma((3, NB, NZ)),
            dma((3, NB, NZ)),
            dma((2, NB)),
            dma((2, NB)),
            dma((GROUPS,)),
            dma((GROUPS,)),
            dma((2,)),
            dma((2,)),
            dma((3,)),
        ],
        compiler_params=pltpu.CompilerParams(
            collective_id=0, has_side_effects=True, vmem_limit_bytes=56 * 2**20),
        cost_estimate=pl.CostEstimate(flops=7 * 10**9, bytes_accessed=12 * 10**6, transcendentals=0),
    )(activations, upstream, momentum, positions, jnp.asarray(cosine_parts()))
    tile = pl.BlockSpec((STRIP, KC), lambda i: (i, 0))
    deep = pl.BlockSpec((1, STRIP, KC), lambda i: (0, i, 0))
    return pl.pallas_call(
        finish,
        grid=(ROWS // STRIP,),
        out_shape=(
            jax.ShapeDtypeStruct((1, ROWS, KC), F32),
            jax.ShapeDtypeStruct((ROWS, KC), F32),
        ),
        in_specs=[deep, tile, pl.BlockSpec((8, HALF), lambda i: (0, 0))],
        out_specs=(deep, tile),
    )(moved, comb, width)


def solution(mesh):
    placed = (
        P("dp", "fsdp", None),
        P("dp", "fsdp", None),
        P("dp", "fsdp", None),
        P(None, "fsdp", None, None),
    )
    return jax.shard_map(
        local,
        mesh=mesh,
        in_specs=placed,
        out_specs=(P("dp", "fsdp", None), P("fsdp", None)),
        check_vma=False,
    )
```

```python
import math

import jax
import jax.numpy as jnp
import ml_dtypes
import numpy as np
from jax import lax
from jax.experimental import pallas as pl
from jax.experimental.pallas import tpu as pltpu
from jax.sharding import PartitionSpec as P

D = 8192
KC = 1024
CH = 64
TOK = 384
GROUPS = 8
NX = 4
NZ = 8
ROWS = 256
HALF = 128
SPAN = NZ * ROWS
FIRST_C = 2
EARLY_C = 4
AHEAD_C = 3
LAG = 2
NB = 1
STRIP = 128
WIDE = KC // NB
LIMIT = math.sqrt(D * KC)
MESH = pl.DeviceIdType.MESH
F32 = jnp.float32
BF16 = jnp.bfloat16
NT = (((1,), (1,)), ((), ()))
TN = (((0,), (0,)), ((), ()))


def cosine_parts():
    k = np.arange(CH, dtype=np.float64)[:, None]
    n = np.arange(CH, dtype=np.float64)[None, :]
    s = np.where(k == 0, math.sqrt(1.0 / CH), math.sqrt(2.0 / CH))
    c = s * np.cos(math.pi * (2.0 * n + 1.0) * k / (2.0 * CH))
    wide = np.kron(np.eye(4), c)
    high = wide.astype(ml_dtypes.bfloat16)
    low = (wide - high.astype(np.float64)).astype(ml_dtypes.bfloat16)
    return np.stack([high, low, high.T, low.T])


def split(x):
    high = x.astype(BF16)
    return high, (x - high.astype(F32)).astype(BF16)


def dot(a, b):
    return jnp.dot(a, b, preferred_element_type=F32)


def kernel(a_ref, u_ref, m_ref, raw_ref, cos_hbm, mom_ref, upd_ref, width_ref,
           own_pos, pos_t, val_t, own_cone, cos_ref, raw,
           ra, rc, ua, ata, atc, part, sbuf, rbuf, ssc, rsc, fbuf, fsc, grad, xg, xm, mask, mom, own, cone,
           vals, vg, vm, norm, spread, asend, arecv, bsend, brecv, blocal, usend, urecv, psend, precv,
           zsend, zrecv, csend, crecv, fsend, frecv, vsend, vrecv, nsend, nrecv, lsem):
    d = lax.axis_index("dp")
    f = lax.axis_index("fsdp")
    x = f // NZ
    z = f % NZ

    core = d % 2
    way = 1 - 2 * core

    def flip(v, j):
        if j == 1:
            return v + 1 - 2 * (v % 2)
        return (v + 2) % NX if j == 2 else NX - 1 - v

    def pick(v, p):
        return flip(v, 1) + p * (flip(v, 3) - flip(v, 1))

    def at_x(v):
        return {"dp": d, "fsdp": v * NZ + z}

    def xpeer(j):
        return at_x(flip(x, j))

    def zpeer(dz):
        return {"dp": d, "fsdp": x * NZ + (z + dz + NZ) % NZ}

    def gpeer(i):
        return {"dp": (d + i) % GROUPS, "fsdp": f}

    def fpeer(i):
        return {"dp": d, "fsdp": (f + i) % (NX * NZ)}

    barrier = pltpu.get_barrier_semaphore()
    peers = [xpeer(i) for i in range(1, NX)] + [zpeer(-way)]
    peers += [gpeer(i) for i in range(1, GROUPS)]
    for peer in peers:
        pl.semaphore_signal(barrier, inc=1, device_id=peer, device_id_type=MESH)

    def chunk(s):
        return (z - way * (1 + s) + 2 * NZ) % NZ

    def pairing(s):
        return (chunk(s) + core) % 2

    def cols(quarter, s, h):
        start = quarter * SPAN + chunk(s) * ROWS + h * HALF
        return pl.ds(pl.multiple_of(start, HALF), HALF)

    def a_copy(j, s):
        return pltpu.make_async_remote_copy(
            src_ref=a_ref.at[0, :, cols(flip(x, j), s, 0)], dst_ref=ra.at[s, j],
            send_sem=asend.at[j, s], recv_sem=arecv.at[j, s], device_id=xpeer(j), device_id_type=MESH)

    def a_local(s):
        return pltpu.make_async_copy(a_ref.at[0, :, cols(x, s, 0)], ra.at[s, 0], arecv.at[0, s])

    def c_copy(q, s):
        p = pairing(s)
        near = pick(x, p)
        quarter = near if q == 1 else pick(near, 1 - p)
        return pltpu.make_async_remote_copy(
            src_ref=a_ref.at[0, :, cols(quarter, s, 1)], dst_ref=rc.at[s, 1, q],
            send_sem=bsend.at[q, s], recv_sem=brecv.at[q, s], device_id=at_x(near), device_id_type=MESH)

    def c_local(q, s):
        quarter = x if q == 1 else pick(x, 1 - pairing(s))
        return pltpu.make_async_copy(a_ref.at[0, :, cols(quarter, s, 1)], rc.at[s, 0, q], blocal.at[q, s])

    def u_copy(j):
        return pltpu.make_async_remote_copy(
            src_ref=u_ref.at[0], dst_ref=ua.at[j], send_sem=usend.at[j], recv_sem=urecv.at[j],
            device_id=xpeer(j), device_id_type=MESH)

    def u_pass(j):
        rows = pl.ds(0, TOK // 2) if j == 1 else pl.ds(TOK // 2, TOK // 2)
        return pltpu.make_async_remote_copy(
            src_ref=ua.at[4 - j, rows], dst_ref=ua.at[2, rows], send_sem=psend.at[j], recv_sem=precv.at[j],
            device_id=xpeer(j), device_id_type=MESH)

    def pair_of(data, scale, device):
        return [
            pltpu.make_async_remote_copy(
                src_ref=src, dst_ref=dst, send_sem=ss, recv_sem=rs, device_id=device, device_id_type=MESH)
            for src, dst, ss, rs in (data, scale)]

    def z_copies(w, b, s):
        return pair_of(
            (sbuf.at[w, b, s], rbuf.at[w, b, s + 1], zsend.at[w, b, s], zrecv.at[w, b, s + 1]),
            (ssc.at[w, b, s], rsc.at[w, b, s + 1], csend.at[w, b, s], crecv.at[w, b, s + 1]),
            zpeer(way))

    def far_copies(b):
        return pair_of(
            (fbuf.at[0, b], fbuf.at[1, b], fsend.at[0, b], frecv.at[0, b]),
            (fsc.at[0, b], fsc.at[1, b], fsend.at[1, b], frecv.at[1, b]),
            at_x(pick(x, 1 - pairing(NZ - 1))))

    u_local = pltpu.make_async_copy(u_ref.at[0], ua.at[0], urecv.at[0])
    u_local.start()
    m_local = pltpu.make_async_copy(m_ref.at[0], mom, lsem.at[0])
    m_local.start()

    cos_local = pltpu.make_async_copy(cos_hbm, cos_ref, lsem.at[1])
    cos_local.start()
    raw_local = pltpu.make_async_copy(raw_ref, raw, lsem.at[2])
    raw_local.start()

    def start_local(s, c):
        for q in range(2):
            c_local(q, s).start()
        a_local(s).start()
        return c

    lax.fori_loop(0, NZ, start_local, 0)

    pl.semaphore_wait(barrier, len(peers))

    for j in (1, 3):
        u_copy(j).start()

    def start_c(s, c):
        for q in range(2):
            c_copy(q, s).start()
        return c

    def start_a(s, c):
        for j in (1, 3, 2):
            a_copy(j, s).start()
        return c

    lax.fori_loop(0, FIRST_C, start_c, 0)

    def clear(i, c):
        for w in range(3):
            for b in range(NB):
                rbuf[w, b, 0, pl.ds(pl.multiple_of(i * 16, 16), 16), :] = jnp.zeros((16, WIDE), jnp.int16)
        return c

    lax.fori_loop(0, HALF // 16, clear, 0)
    for w in range(3):
        for b in range(NB):
            rsc[w, b, 0] = jnp.zeros((8, HALF), F32)

    raw_local.wait()
    for a in range(4):
        rows = slice(a * 4, (a + 1) * 4)
        own_pos[rows, :] = jnp.concatenate([raw[d, a, pl.ds(m, 4, stride=4), :] for m in range(4)], axis=1)
        for m in range(4):
            pos_t[m, rows, :] = jnp.concatenate(
                [raw[g, a, pl.ds(m, 4, stride=4), :] for g in range(GROUPS)], axis=1)

    def one_hot_columns(q, c):
        wide = lax.broadcasted_iota(jnp.int32, (ROWS, HALF), 0)
        lane = lax.broadcasted_iota(jnp.int32, (1, HALF), 1)
        col = (own_pos[pl.ds(q, 1), :] & (CH - 1)) + (lane >> 5) * CH
        own_cone[q] = jnp.where(wide == col, 1.0, 0.0).astype(BF16)
        short = lax.broadcasted_iota(jnp.int32, (CH, ROWS), 0)
        for m in range(4):
            hit = short == (pos_t[m, pl.ds(q, 1), :] & (CH - 1))
            cone[q, m * CH:(m + 1) * CH, :] = jnp.where(hit, 1.0, 0.0).astype(BF16)
        return c

    lax.fori_loop(0, 16, one_hot_columns, 0)

    def quad(ref, q):
        rows = pl.ds(pl.multiple_of(q // 4 * CH, CH), CH)
        return ref.at[rows, pl.ds(pl.multiple_of(q % 4 * ROWS, ROWS), ROWS)]

    def own_columns(q):
        return own_cone[q]

    def own_rows(q):
        tall = lax.broadcasted_iota(jnp.int32, (CH, HALF), 0)
        return jnp.where(tall == (own_pos[pl.ds(q, 1), :] >> 6), 1.0, 0.0).astype(BF16)

    def build_mask(q, c):
        quad(mask, q)[...] = lax.dot_general(own_rows(q), own_columns(q), NT, preferred_element_type=F32)
        return c

    lax.fori_loop(0, 16, build_mask, 0)

    def transform(src, dst, left, right):
        def body(j, c):
            at_cols = pl.ds(pl.multiple_of(j * ROWS, ROWS), ROWS)
            h, l = split(src[:, at_cols])
            tall = jnp.concatenate([cos_ref[left], cos_ref[left], cos_ref[left + 1]], axis=1)
            h, l = split(dot(tall, jnp.concatenate([h, l, h], axis=0)))
            deep = jnp.concatenate([cos_ref[right], cos_ref[right], cos_ref[right + 1]], axis=0)
            dst[:, at_cols] = dot(jnp.concatenate([h, l, h], axis=1), deep)
            return c

        lax.fori_loop(0, KC // ROWS, body, 0)

    def gather(src, dst):
        def body(q, c):
            h, l = split(quad(src, q)[...])
            r = own_rows(q)
            t = (lax.dot_general(h, r, TN, preferred_element_type=F32)
                 + lax.dot_general(l, r, TN, preferred_element_type=F32))
            dst[pl.ds(q, 1), :] = jnp.sum(t * own_columns(q).astype(F32), axis=0, keepdims=True)
            return c

        lax.fori_loop(0, 16, body, 0)

    m_local.wait()
    cos_local.wait()
    transform(mom, xm, 0, 2)
    gather(xm, vm)

    u_local.wait()
    for j in (1, 3):
        u_copy(j).wait_recv()
    for j in (1, 3):
        u_pass(j).start()
    lax.fori_loop(FIRST_C, EARLY_C, start_c, 0)

    def product_c(s):
        for q in range(2):
            c_local(q, s).wait()
            c_copy(q, s).wait_recv()
        for q in range(2):
            for k in range(2):
                atc[q * HALF:(q + 1) * HALF, k * TOK:(k + 1) * TOK] = rc[s, k, q].T
        near = 1 + 2 * pairing(s)

        def body(j, c):
            here = pl.ds(pl.multiple_of(j * ROWS, ROWS), ROWS)
            both = jnp.concatenate([ua[0, :, here], ua[near, :, here]], axis=0)
            part[0:ROWS, here] = dot(atc[...], both)
            return c

        lax.fori_loop(0, KC // ROWS, body, 0)

    def product_a(s):
        a_local(s).wait()
        for j in range(1, NX):
            a_copy(j, s).wait_recv()
        for j in range(NX):
            ata[:, j * TOK:(j + 1) * TOK] = ra[s, j].T

        def body(j, c):
            here = pl.ds(pl.multiple_of(j * ROWS, ROWS), ROWS)
            part[ROWS:ROWS + HALF, here] = dot(ata[...], ua[:, :, here].reshape(NX * TOK, ROWS))
            return c

        lax.fori_loop(0, KC // ROWS, body, 0)

    def encode(v, codes, scales, j, here):
        top = jnp.maximum(jnp.max(jnp.abs(v), axis=0, keepdims=True), 1e-30)
        scales[pl.ds(j, 1), :] = top * (1.0 / 32767.0)
        code = lax.round(v * (32767.0 / top), lax.RoundingMethod.TO_NEAREST_EVEN)
        codes[:, here] = code.astype(jnp.int32).astype(jnp.int16)

    def reduce_step(w, s, last):
        for b in range(NB):
            @pl.when(s > 0)
            def _():
                for copy in z_copies(w, b, s - 1):
                    copy.wait_recv()

            def body(j, c):
                here = pl.ds(pl.multiple_of(j * HALF, HALF), HALF)
                there = pl.ds(pl.multiple_of(b * WIDE + j * HALF, HALF), HALF)
                v = part[w * HALF:(w + 1) * HALF, there]
                v += rbuf[w, b, s, :, here].astype(F32) * rsc[w, b, s, pl.ds(j, 1), :]
                if not last:
                    encode(v, sbuf.at[w, b, s], ssc.at[w, b, s], j, here)
                elif w == 0:
                    encode(v, fbuf.at[0, b], fsc.at[0, b], j, here)
                else:
                    top = HALF * (w % 2)
                    grad[top:top + HALF, there] = v
                return c

            lax.fori_loop(0, WIDE // HALF, body, 0)
            if not last:
                for copy in z_copies(w, b, s):
                    copy.start()
            elif w == 0:
                for copy in far_copies(b):
                    copy.start()

    def step_c(s, last):
        product_c(s)
        reduce_step(0, s, last)
        reduce_step(1, s, last)

    def step_a(s, last):
        product_a(s)
        reduce_step(2, s, last)

    def only_c(t, c):
        step_c(t, False)
        start_a(t, 0)
        return c

    def mixed(t, c):
        @pl.when(t + AHEAD_C < NZ)
        def _():
            start_c(t + AHEAD_C, 0)
        start_a(t, 0)
        step_c(t, False)
        step_a(t - LAG, False)
        return c

    def only_a(t, c):
        step_a(t - LAG, False)
        return c

    lax.fori_loop(0, LAG, only_c, 0)
    start_c(EARLY_C, 0)
    for j in (1, 3):
        u_pass(j).wait_recv()
    lax.fori_loop(LAG, NZ - 1, mixed, 0)
    start_a(NZ - 1, 0)
    step_c(NZ - 1, True)
    lax.fori_loop(NZ - 1, NZ - 1 + LAG, only_a, 0)
    step_a(NZ - 1, True)

    for b in range(NB):
        for copy in far_copies(b):
            copy.wait_recv()

        def add_far(j, c):
            here = pl.ds(pl.multiple_of(j * HALF, HALF), HALF)
            there = pl.ds(pl.multiple_of(b * WIDE + j * HALF, HALF), HALF)
            grad[HALF:ROWS, there] += fbuf[1, b, :, here].astype(F32) * fsc[1, b, pl.ds(j, 1), :]
            return c

        lax.fori_loop(0, WIDE // HALF, add_far, 0)

    def spread_copy(e, buf, i):
        return pltpu.make_async_remote_copy(
            src_ref=buf.at[f], dst_ref=buf.at[f], send_sem=nsend.at[e], recv_sem=nrecv.at[e],
            device_id=fpeer(i), device_id_type=MESH)

    def all_copies(e, buf):
        others = buf.at[pl.ds(0, NX * NZ - 1)]
        return pltpu.make_async_remote_copy(
            src_ref=others, dst_ref=others, send_sem=nsend.at[e], recv_sem=nrecv.at[e],
            device_id=fpeer(1), device_id_type=MESH)

    def share(e, buf):
        def go(i, c):
            spread_copy(e, buf, i).start()
            return c

        lax.fori_loop(1, NX * NZ, go, 0)

    def shared(e, buf):
        all_copies(e, buf).wait_recv()
        return jnp.sum(jnp.sum(buf[...], axis=0), keepdims=True)

    def squares(ref):
        def body(i, acc):
            v = ref[pl.ds(pl.multiple_of(i * 8, 8), 8), :]
            return acc + v * v

        acc = lax.fori_loop(0, ROWS // 8, body, jnp.zeros((8, KC), F32))
        total = acc[:, 0:HALF]
        for j in range(1, KC // HALF):
            total += acc[:, j * HALF:(j + 1) * HALF]
        return jnp.sum(total, axis=0, keepdims=True)

    norm[f] = squares(grad)
    share(0, norm)
    transform(grad, xg, 0, 2)
    gather(xg, vg)

    def x_sent(s, c):
        for j in range(1, NX):
            a_copy(j, s).wait_send()
        for q in range(2):
            c_copy(q, s).wait_send()
        return c

    def z_sent(s, c):
        for w in range(3):
            for b in range(NB):
                for copy in z_copies(w, b, s):
                    copy.wait_send()
        return c

    lax.fori_loop(0, NZ, x_sent, 0)
    lax.fori_loop(0, NZ - 1, z_sent, 0)
    for j in (1, 3):
        u_copy(j).wait_send()
        u_pass(j).wait_send()
    for b in range(NB):
        for copy in far_copies(b):
            copy.wait_send()
    all_copies(0, norm).wait_send()
    total = shared(0, norm)
    factor = LIMIT / jnp.maximum(jnp.sqrt(total), LIMIT)

    vals[d] = 0.999 * vm[...] + factor * vg[...]

    def v_copy(i, target):
        return pltpu.make_async_remote_copy(
            src_ref=vals.at[d], dst_ref=vals.at[target], send_sem=vsend.at[i], recv_sem=vrecv.at[i],
            device_id=gpeer(i), device_id_type=MESH)

    for i in range(1, GROUPS):
        v_copy(i, d).start()

    xg[...] = mask[...] * (0.999 * xm[...] + factor * xg[...])
    transform(xg, own, 2, 0)
    mom[...] = 0.999 * mom[...] + factor * grad[...] - own[...]
    mom_out = pltpu.make_async_copy(mom, mom_ref.at[0], lsem.at[0])
    mom_out.start()

    for i in range(1, GROUPS):
        v_copy(i, (d - i + GROUPS) % GROUPS).wait_recv()

    for m in range(4):
        val_t[m] = jnp.concatenate([vals[g, :, m * 32:(m + 1) * 32] for g in range(GROUPS)], axis=1)

    def scatter(q, c):
        tall = lax.broadcasted_iota(jnp.int32, (CH, ROWS), 0)
        pieces = []
        for m in range(4):
            hit = tall == (pos_t[m, pl.ds(q, 1), :] >> 6)
            pieces += split(jnp.where(hit, val_t[m, pl.ds(q, 1), :], 0.0))
        every = lax.dot_general(jnp.concatenate(pieces, axis=0), cone[q], NT, preferred_element_type=F32)
        block = lax.broadcasted_iota(jnp.int32, (CH, ROWS), 1) >> 6
        total = jnp.zeros((CH, ROWS), F32)
        for m in range(4):
            both = every[m * HALF:m * HALF + CH] + every[m * HALF + CH:(m + 1) * HALF]
            total = jnp.where(block == m, both, total)
        quad(xm, q)[...] = total * (1.0 / GROUPS)
        return c

    lax.fori_loop(0, 16, scatter, 0)
    spread[f] = squares(xm)
    share(1, spread)
    transform(xm, own, 2, 0)
    upd_out = pltpu.make_async_copy(own, upd_ref, lsem.at[1])
    upd_out.start()
    width = jnp.sqrt(shared(1, spread) / (D * KC) + 1e-6)
    width_ref[...] = jnp.broadcast_to(1.0 / (0.5 * width), (8, HALF))

    all_copies(1, spread).wait_send()
    for i in range(1, GROUPS):
        v_copy(i, d).wait_send()
    mom_out.wait()
    upd_out.wait()


def finish(mom_in, comb_in, width_in, mom_out, upd_out):
    mom_out[...] = mom_in[...]
    upd_out[...] = jnp.tanh(comb_in[...] * width_in[0:1, 0:1])


def local(activations, upstream, momentum, positions):
    dma = pltpu.SemaphoreType.DMA
    hbm = pl.BlockSpec(memory_space=pl.ANY)
    vmem = pl.BlockSpec(memory_space=pltpu.VMEM)
    moved, comb, width = pl.pallas_call(
        kernel,
        out_shape=(
            jax.ShapeDtypeStruct((1, ROWS, KC), F32),
            jax.ShapeDtypeStruct((ROWS, KC), F32),
            jax.ShapeDtypeStruct((8, HALF), F32),
        ),
        in_specs=[hbm] * 5,
        out_specs=(hbm, hbm, vmem),
        scratch_shapes=[
            pltpu.VMEM((16, HALF), jnp.int32),
            pltpu.VMEM((4, 16, ROWS), jnp.int32),
            pltpu.VMEM((4, 16, ROWS), F32),
            pltpu.VMEM((16, ROWS, HALF), BF16),
            pltpu.VMEM((4, ROWS, ROWS), BF16),
            pltpu.VMEM((GROUPS, 4, 16, 32), jnp.int32),
            pltpu.VMEM((NZ, NX, TOK, HALF), BF16),
            pltpu.VMEM((NZ, 2, 2, TOK, HALF), BF16),
            pltpu.VMEM((NX, TOK, KC), BF16),
            pltpu.VMEM((HALF, NX * TOK), BF16),
            pltpu.VMEM((ROWS, 2 * TOK), BF16),
            pltpu.VMEM((ROWS + HALF, KC), F32),
            pltpu.VMEM((3, NB, NZ - 1, HALF, WIDE), jnp.int16),
            pltpu.VMEM((3, NB, NZ, HALF, WIDE), jnp.int16),
            pltpu.VMEM((3, NB, NZ - 1, 8, HALF), F32),
            pltpu.VMEM((3, NB, NZ, 8, HALF), F32),
            pltpu.VMEM((2, NB, HALF, WIDE), jnp.int16),
            pltpu.VMEM((2, NB, 8, HALF), F32),
            pltpu.VMEM((ROWS, KC), F32),
            pltpu.VMEM((ROWS, KC), F32),
            pltpu.VMEM((ROWS, KC), F32),
            pltpu.VMEM((ROWS, KC), F32),
            pltpu.VMEM((ROWS, KC), F32),
            pltpu.VMEM((ROWS, KC), F32),
            pltpu.VMEM((16, ROWS, ROWS), BF16),
            pltpu.VMEM((GROUPS, 16, HALF), F32),
            pltpu.VMEM((16, HALF), F32),
            pltpu.VMEM((16, HALF), F32),
            pltpu.VMEM((NX * NZ, 1, HALF), F32),
            pltpu.VMEM((NX * NZ, 1, HALF), F32),
            dma((NX, NZ)),
            dma((NX, NZ)),
            dma((2, NZ)),
            dma((2, NZ)),
            dma((2, NZ)),
            dma((NX,)),
            dma((NX,)),
            dma((NX,)),
            dma((NX,)),
            dma((3, NB, NZ)),
            dma((3, NB, NZ)),
            dma((3, NB, NZ)),
            dma((3, NB, NZ)),
            dma((2, NB)),
            dma((2, NB)),
            dma((GROUPS,)),
            dma((GROUPS,)),
            dma((2,)),
            dma((2,)),
            dma((3,)),
        ],
        compiler_params=pltpu.CompilerParams(
            collective_id=0, has_side_effects=True, vmem_limit_bytes=56 * 2**20),
        cost_estimate=pl.CostEstimate(flops=7 * 10**9, bytes_accessed=12 * 10**6, transcendentals=0),
    )(activations, upstream, momentum, positions, jnp.asarray(cosine_parts()))
    tile = pl.BlockSpec((STRIP, KC), lambda i: (i, 0))
    deep = pl.BlockSpec((1, STRIP, KC), lambda i: (0, i, 0))
    return pl.pallas_call(
        finish,
        grid=(ROWS // STRIP,),
        out_shape=(
            jax.ShapeDtypeStruct((1, ROWS, KC), F32),
            jax.ShapeDtypeStruct((ROWS, KC), F32),
        ),
        in_specs=[deep, tile, pl.BlockSpec((8, HALF), lambda i: (0, 0))],
        out_specs=(deep, tile),
    )(moved, comb, width)


def solution(mesh):
    placed = (
        P("dp", "fsdp", None),
        P("dp", "fsdp", None),
        P("dp", "fsdp", None),
        P(None, "fsdp", None, None),
    )
    return jax.shard_map(
        local,
        mesh=mesh,
        in_specs=placed,
        out_specs=(P("dp", "fsdp", None), P("fsdp", None)),
        check_vma=False,
    )
```

```python
import math

import jax
import jax.numpy as jnp
import ml_dtypes
import numpy as np
from jax import lax
from jax.experimental import pallas as pl
from jax.experimental.pallas import tpu as pltpu
from jax.sharding import PartitionSpec as P

D = 8192
KC = 1024
CH = 64
TOK = 384
GROUPS = 8
NX = 4
NZ = 8
ROWS = 256
HALF = 128
SPAN = NZ * ROWS
FIRST_C = 1
EARLY_C = 4
AHEAD_C = 3
LAG = 2
NB = 2
STRIP = 128
WIDE = KC // NB
LIMIT = math.sqrt(D * KC)
MESH = pl.DeviceIdType.MESH
F32 = jnp.float32
BF16 = jnp.bfloat16
NT = (((1,), (1,)), ((), ()))
TN = (((0,), (0,)), ((), ()))


def cosine_parts():
    k = np.arange(CH, dtype=np.float64)[:, None]
    n = np.arange(CH, dtype=np.float64)[None, :]
    s = np.where(k == 0, math.sqrt(1.0 / CH), math.sqrt(2.0 / CH))
    c = s * np.cos(math.pi * (2.0 * n + 1.0) * k / (2.0 * CH))
    wide = np.kron(np.eye(4), c)
    high = wide.astype(ml_dtypes.bfloat16)
    low = (wide - high.astype(np.float64)).astype(ml_dtypes.bfloat16)
    return np.stack([high, low, high.T, low.T])


def split(x):
    high = x.astype(BF16)
    return high, (x - high.astype(F32)).astype(BF16)


def dot(a, b):
    return jnp.dot(a, b, preferred_element_type=F32)


def kernel(a_ref, u_ref, m_ref, raw_ref, cos_hbm, mom_ref, upd_ref, width_ref,
           own_pos, pos_t, val_t, own_cone, cos_ref, raw,
           ra, rc, ua, ata, atc, part, sbuf, rbuf, ssc, rsc, fbuf, fsc, grad, xg, xm, mask, mom, own, cone,
           vals, vg, vm, norm, spread, asend, arecv, bsend, brecv, blocal, usend, urecv, psend, precv,
           zsend, zrecv, csend, crecv, fsend, frecv, vsend, vrecv, nsend, nrecv, lsem):
    d = lax.axis_index("dp")
    f = lax.axis_index("fsdp")
    x = f // NZ
    z = f % NZ

    core = d % 2
    way = 1 - 2 * core

    def flip(v, j):
        if j == 1:
            return v + 1 - 2 * (v % 2)
        return (v + 2) % NX if j == 2 else NX - 1 - v

    def pick(v, p):
        return flip(v, 1) + p * (flip(v, 3) - flip(v, 1))

    def at_x(v):
        return {"dp": d, "fsdp": v * NZ + z}

    def xpeer(j):
        return at_x(flip(x, j))

    def zpeer(dz):
        return {"dp": d, "fsdp": x * NZ + (z + dz + NZ) % NZ}

    def gpeer(i):
        return {"dp": (d + i) % GROUPS, "fsdp": f}

    def fpeer(i):
        return {"dp": d, "fsdp": (f + i) % (NX * NZ)}

    barrier = pltpu.get_barrier_semaphore()
    peers = [xpeer(i) for i in range(1, NX)] + [zpeer(-way)]
    peers += [gpeer(i) for i in range(1, GROUPS)]
    for peer in peers:
        pl.semaphore_signal(barrier, inc=1, device_id=peer, device_id_type=MESH)

    def chunk(s):
        return (z - way * (1 + s) + 2 * NZ) % NZ

    def pairing(s):
        return (chunk(s) + core) % 2

    def cols(quarter, s, h):
        start = quarter * SPAN + chunk(s) * ROWS + h * HALF
        return pl.ds(pl.multiple_of(start, HALF), HALF)

    def a_copy(j, s):
        return pltpu.make_async_remote_copy(
            src_ref=a_ref.at[0, :, cols(flip(x, j), s, 0)], dst_ref=ra.at[s, j],
            send_sem=asend.at[j, s], recv_sem=arecv.at[j, s], device_id=xpeer(j), device_id_type=MESH)

    def a_local(s):
        return pltpu.make_async_copy(a_ref.at[0, :, cols(x, s, 0)], ra.at[s, 0], arecv.at[0, s])

    def c_copy(q, s):
        p = pairing(s)
        near = pick(x, p)
        quarter = near if q == 1 else pick(near, 1 - p)
        return pltpu.make_async_remote_copy(
            src_ref=a_ref.at[0, :, cols(quarter, s, 1)], dst_ref=rc.at[s, 1, q],
            send_sem=bsend.at[q, s], recv_sem=brecv.at[q, s], device_id=at_x(near), device_id_type=MESH)

    def c_local(q, s):
        quarter = x if q == 1 else pick(x, 1 - pairing(s))
        return pltpu.make_async_copy(a_ref.at[0, :, cols(quarter, s, 1)], rc.at[s, 0, q], blocal.at[q, s])

    def u_copy(j):
        return pltpu.make_async_remote_copy(
            src_ref=u_ref.at[0], dst_ref=ua.at[j], send_sem=usend.at[j], recv_sem=urecv.at[j],
            device_id=xpeer(j), device_id_type=MESH)

    def u_pass(j):
        rows = pl.ds(0, TOK // 2) if j == 1 else pl.ds(TOK // 2, TOK // 2)
        return pltpu.make_async_remote_copy(
            src_ref=ua.at[4 - j, rows], dst_ref=ua.at[2, rows], send_sem=psend.at[j], recv_sem=precv.at[j],
            device_id=xpeer(j), device_id_type=MESH)

    def pair_of(data, scale, device):
        return [
            pltpu.make_async_remote_copy(
                src_ref=src, dst_ref=dst, send_sem=ss, recv_sem=rs, device_id=device, device_id_type=MESH)
            for src, dst, ss, rs in (data, scale)]

    def z_copies(w, b, s):
        return pair_of(
            (sbuf.at[w, b, s], rbuf.at[w, b, s + 1], zsend.at[w, b, s], zrecv.at[w, b, s + 1]),
            (ssc.at[w, b, s], rsc.at[w, b, s + 1], csend.at[w, b, s], crecv.at[w, b, s + 1]),
            zpeer(way))

    def far_copies(b):
        return pair_of(
            (fbuf.at[0, b], fbuf.at[1, b], fsend.at[0, b], frecv.at[0, b]),
            (fsc.at[0, b], fsc.at[1, b], fsend.at[1, b], frecv.at[1, b]),
            at_x(pick(x, 1 - pairing(NZ - 1))))

    u_local = pltpu.make_async_copy(u_ref.at[0], ua.at[0], urecv.at[0])
    u_local.start()
    m_local = pltpu.make_async_copy(m_ref.at[0], mom, lsem.at[0])
    m_local.start()

    cos_local = pltpu.make_async_copy(cos_hbm, cos_ref, lsem.at[1])
    cos_local.start()
    raw_local = pltpu.make_async_copy(raw_ref, raw, lsem.at[2])
    raw_local.start()

    def start_local(s, c):
        for q in range(2):
            c_local(q, s).start()
        a_local(s).start()
        return c

    lax.fori_loop(0, NZ, start_local, 0)

    pl.semaphore_wait(barrier, len(peers))

    for j in (1, 3):
        u_copy(j).start()

    def start_c(s, c):
        for q in range(2):
            c_copy(q, s).start()
        return c

    def start_a(s, c):
        for j in (1, 3, 2):
            a_copy(j, s).start()
        return c

    lax.fori_loop(0, FIRST_C, start_c, 0)

    def clear(i, c):
        for w in range(3):
            for b in range(NB):
                rbuf[w, b, 0, pl.ds(pl.multiple_of(i * 16, 16), 16), :] = jnp.zeros((16, WIDE), jnp.int16)
        return c

    lax.fori_loop(0, HALF // 16, clear, 0)
    ssc[...] = jnp.zeros(ssc.shape, F32)
    fsc[0] = jnp.zeros(fsc.shape[1:], F32)
    for w in range(3):
        for b in range(NB):
            rsc[w, b, 0] = jnp.zeros((8, HALF), F32)

    raw_local.wait()
    for a in range(4):
        rows = slice(a * 4, (a + 1) * 4)
        own_pos[rows, :] = jnp.concatenate([raw[d, a, pl.ds(m, 4, stride=4), :] for m in range(4)], axis=1)
        for m in range(4):
            pos_t[m, rows, :] = jnp.concatenate(
                [raw[g, a, pl.ds(m, 4, stride=4), :] for g in range(GROUPS)], axis=1)

    def one_hot_columns(q, c):
        wide = lax.broadcasted_iota(jnp.int32, (ROWS, HALF), 0)
        lane = lax.broadcasted_iota(jnp.int32, (1, HALF), 1)
        col = (own_pos[pl.ds(q, 1), :] & (CH - 1)) + (lane >> 5) * CH
        own_cone[q] = jnp.where(wide == col, 1.0, 0.0).astype(BF16)
        short = lax.broadcasted_iota(jnp.int32, (CH, ROWS), 0)
        for m in range(4):
            hit = short == (pos_t[m, pl.ds(q, 1), :] & (CH - 1))
            cone[q, m * CH:(m + 1) * CH, :] = jnp.where(hit, 1.0, 0.0).astype(BF16)
        return c

    lax.fori_loop(0, 16, one_hot_columns, 0)

    def quad(ref, q):
        rows = pl.ds(pl.multiple_of(q // 4 * CH, CH), CH)
        return ref.at[rows, pl.ds(pl.multiple_of(q % 4 * ROWS, ROWS), ROWS)]

    def own_columns(q):
        return own_cone[q]

    def own_rows(q):
        tall = lax.broadcasted_iota(jnp.int32, (CH, HALF), 0)
        return jnp.where(tall == (own_pos[pl.ds(q, 1), :] >> 6), 1.0, 0.0).astype(BF16)

    def build_mask(q, c):
        quad(mask, q)[...] = lax.dot_general(own_rows(q), own_columns(q), NT, preferred_element_type=F32)
        return c

    lax.fori_loop(0, 16, build_mask, 0)

    def transform(src, dst, left, right):
        def body(j, c):
            at_cols = pl.ds(pl.multiple_of(j * ROWS, ROWS), ROWS)
            h, l = split(src[:, at_cols])
            tall = jnp.concatenate([cos_ref[left], cos_ref[left], cos_ref[left + 1]], axis=1)
            h, l = split(dot(tall, jnp.concatenate([h, l, h], axis=0)))
            deep = jnp.concatenate([cos_ref[right], cos_ref[right], cos_ref[right + 1]], axis=0)
            dst[:, at_cols] = dot(jnp.concatenate([h, l, h], axis=1), deep)
            return c

        lax.fori_loop(0, KC // ROWS, body, 0)

    def gather(src, dst):
        def body(q, c):
            h, l = split(quad(src, q)[...])
            r = own_rows(q)
            t = (lax.dot_general(h, r, TN, preferred_element_type=F32)
                 + lax.dot_general(l, r, TN, preferred_element_type=F32))
            dst[pl.ds(q, 1), :] = jnp.sum(t * own_columns(q).astype(F32), axis=0, keepdims=True)
            return c

        lax.fori_loop(0, 16, body, 0)

    m_local.wait()
    cos_local.wait()
    transform(mom, xm, 0, 2)
    gather(xm, vm)

    u_local.wait()
    for j in (1, 3):
        u_copy(j).wait_recv()
    for j in (1, 3):
        u_pass(j).start()
    lax.fori_loop(FIRST_C, EARLY_C, start_c, 0)

    def product_c(s):
        for q in range(2):
            c_local(q, s).wait()
            c_copy(q, s).wait_recv()
        for q in range(2):
            for k in range(2):
                atc[q * HALF:(q + 1) * HALF, k * TOK:(k + 1) * TOK] = rc[s, k, q].T
        near = 1 + 2 * pairing(s)

        def body(j, c):
            here = pl.ds(pl.multiple_of(j * ROWS, ROWS), ROWS)
            both = jnp.concatenate([ua[0, :, here], ua[near, :, here]], axis=0)
            part[0:ROWS, here] = dot(atc[...], both)
            return c

        lax.fori_loop(0, KC // ROWS, body, 0)

    def product_a(s):
        a_local(s).wait()
        for j in range(1, NX):
            a_copy(j, s).wait_recv()
        for j in range(NX):
            ata[:, j * TOK:(j + 1) * TOK] = ra[s, j].T

        def body(j, c):
            here = pl.ds(pl.multiple_of(j * ROWS, ROWS), ROWS)
            part[ROWS:ROWS + HALF, here] = dot(ata[...], ua[:, :, here].reshape(NX * TOK, ROWS))
            return c

        lax.fori_loop(0, KC // ROWS, body, 0)

    def encode(v, codes, scales, j, here):
        top = jnp.maximum(jnp.max(jnp.abs(v), axis=0, keepdims=True), 1e-30)
        scales[pl.ds(j, 1), :] = top * (1.0 / 32767.0)
        code = lax.round(v * (32767.0 / top), lax.RoundingMethod.TO_NEAREST_EVEN)
        codes[:, here] = code.astype(jnp.int32).astype(jnp.int16)

    def reduce_step(w, s, last):
        for b in range(NB):
            @pl.when(s > 0)
            def _():
                for copy in z_copies(w, b, s - 1):
                    copy.wait_recv()

            def body(j, c):
                here = pl.ds(pl.multiple_of(j * HALF, HALF), HALF)
                there = pl.ds(pl.multiple_of(b * WIDE + j * HALF, HALF), HALF)
                v = part[w * HALF:(w + 1) * HALF, there]
                v += rbuf[w, b, s, :, here].astype(F32) * rsc[w, b, s, pl.ds(j, 1), :]
                if not last:
                    encode(v, sbuf.at[w, b, s], ssc.at[w, b, s], j, here)
                elif w == 0:
                    encode(v, fbuf.at[0, b], fsc.at[0, b], j, here)
                else:
                    top = HALF * (w % 2)
                    grad[top:top + HALF, there] = v
                return c

            lax.fori_loop(0, WIDE // HALF, body, 0)
            if not last:
                for copy in z_copies(w, b, s):
                    copy.start()
            elif w == 0:
                for copy in far_copies(b):
                    copy.start()

    def step_c(s, last):
        product_c(s)
        reduce_step(0, s, last)
        reduce_step(1, s, last)

    def step_a(s, last):
        product_a(s)
        reduce_step(2, s, last)

    def only_c(t, c):
        step_c(t, False)
        start_a(t, 0)
        return c

    def mixed(t, c):
        @pl.when(t + AHEAD_C < NZ)
        def _():
            start_c(t + AHEAD_C, 0)
        start_a(t, 0)
        step_c(t, False)
        step_a(t - LAG, False)
        return c

    def only_a(t, c):
        step_a(t - LAG, False)
        return c

    lax.fori_loop(0, LAG, only_c, 0)
    start_c(EARLY_C, 0)
    for j in (1, 3):
        u_pass(j).wait_recv()
    lax.fori_loop(LAG, NZ - 1, mixed, 0)
    start_a(NZ - 1, 0)
    step_c(NZ - 1, True)
    lax.fori_loop(NZ - 1, NZ - 1 + LAG, only_a, 0)
    step_a(NZ - 1, True)

    for b in range(NB):
        for copy in far_copies(b):
            copy.wait_recv()

        def add_far(j, c):
            here = pl.ds(pl.multiple_of(j * HALF, HALF), HALF)
            there = pl.ds(pl.multiple_of(b * WIDE + j * HALF, HALF), HALF)
            grad[HALF:ROWS, there] += fbuf[1, b, :, here].astype(F32) * fsc[1, b, pl.ds(j, 1), :]
            return c

        lax.fori_loop(0, WIDE // HALF, add_far, 0)

    def spread_copy(e, buf, i):
        return pltpu.make_async_remote_copy(
            src_ref=buf.at[f], dst_ref=buf.at[f], send_sem=nsend.at[e], recv_sem=nrecv.at[e],
            device_id=fpeer(i), device_id_type=MESH)

    def all_copies(e, buf):
        others = buf.at[pl.ds(0, NX * NZ - 1)]
        return pltpu.make_async_remote_copy(
            src_ref=others, dst_ref=others, send_sem=nsend.at[e], recv_sem=nrecv.at[e],
            device_id=fpeer(1), device_id_type=MESH)

    def share(e, buf):
        def go(i, c):
            spread_copy(e, buf, i).start()
            return c

        lax.fori_loop(1, NX * NZ, go, 0)

    def shared(e, buf):
        all_copies(e, buf).wait_recv()
        return jnp.sum(jnp.sum(buf[...], axis=0), keepdims=True)

    def squares(ref):
        def body(i, acc):
            v = ref[pl.ds(pl.multiple_of(i * 8, 8), 8), :]
            return acc + v * v

        acc = lax.fori_loop(0, ROWS // 8, body, jnp.zeros((8, KC), F32))
        total = acc[:, 0:HALF]
        for j in range(1, KC // HALF):
            total += acc[:, j * HALF:(j + 1) * HALF]
        return jnp.sum(total, axis=0, keepdims=True)

    norm[f] = squares(grad)
    share(0, norm)
    transform(grad, xg, 0, 2)
    gather(xg, vg)

    def x_sent(s, c):
        for j in range(1, NX):
            a_copy(j, s).wait_send()
        for q in range(2):
            c_copy(q, s).wait_send()
        return c

    def z_sent(s, c):
        for w in range(3):
            for b in range(NB):
                for copy in z_copies(w, b, s):
                    copy.wait_send()
        return c

    lax.fori_loop(0, NZ, x_sent, 0)
    lax.fori_loop(0, NZ - 1, z_sent, 0)
    for j in (1, 3):
        u_copy(j).wait_send()
        u_pass(j).wait_send()
    for b in range(NB):
        for copy in far_copies(b):
            copy.wait_send()
    all_copies(0, norm).wait_send()
    total = shared(0, norm)
    factor = LIMIT / jnp.maximum(jnp.sqrt(total), LIMIT)

    vals[d] = 0.999 * vm[...] + factor * vg[...]

    def v_copy(i, target):
        return pltpu.make_async_remote_copy(
            src_ref=vals.at[d], dst_ref=vals.at[target], send_sem=vsend.at[i], recv_sem=vrecv.at[i],
            device_id=gpeer(i), device_id_type=MESH)

    for i in range(1, GROUPS):
        v_copy(i, d).start()

    xg[...] = mask[...] * (0.999 * xm[...] + factor * xg[...])
    transform(xg, own, 2, 0)
    mom[...] = 0.999 * mom[...] + factor * grad[...] - own[...]
    mom_out = pltpu.make_async_copy(mom, mom_ref.at[0], lsem.at[0])
    mom_out.start()

    for i in range(1, GROUPS):
        v_copy(i, (d - i + GROUPS) % GROUPS).wait_recv()

    for m in range(4):
        val_t[m] = jnp.concatenate([vals[g, :, m * 32:(m + 1) * 32] for g in range(GROUPS)], axis=1)

    def scatter(q, c):
        tall = lax.broadcasted_iota(jnp.int32, (CH, ROWS), 0)
        pieces = []
        for m in range(4):
            hit = tall == (pos_t[m, pl.ds(q, 1), :] >> 6)
            pieces += split(jnp.where(hit, val_t[m, pl.ds(q, 1), :], 0.0))
        every = lax.dot_general(jnp.concatenate(pieces, axis=0), cone[q], NT, preferred_element_type=F32)
        block = lax.broadcasted_iota(jnp.int32, (CH, ROWS), 1) >> 6
        total = jnp.zeros((CH, ROWS), F32)
        for m in range(4):
            both = every[m * HALF:m * HALF + CH] + every[m * HALF + CH:(m + 1) * HALF]
            total = jnp.where(block == m, both, total)
        quad(xm, q)[...] = total * (1.0 / GROUPS)
        return c

    lax.fori_loop(0, 16, scatter, 0)
    spread[f] = squares(xm)
    share(1, spread)
    transform(xm, own, 2, 0)
    upd_out = pltpu.make_async_copy(own, upd_ref, lsem.at[1])
    upd_out.start()
    width = jnp.sqrt(shared(1, spread) / (D * KC) + 1e-6)
    width_ref[...] = jnp.broadcast_to(1.0 / (0.5 * width), (8, HALF))

    all_copies(1, spread).wait_send()
    for i in range(1, GROUPS):
        v_copy(i, d).wait_send()
    mom_out.wait()
    upd_out.wait()


def finish(mom_in, comb_in, width_in, mom_out, upd_out):
    mom_out[...] = mom_in[...]
    upd_out[...] = jnp.tanh(comb_in[...] * width_in[0:1, 0:1])


def local(activations, upstream, momentum, positions):
    dma = pltpu.SemaphoreType.DMA
    hbm = pl.BlockSpec(memory_space=pl.ANY)
    vmem = pl.BlockSpec(memory_space=pltpu.VMEM)
    moved, comb, width = pl.pallas_call(
        kernel,
        out_shape=(
            jax.ShapeDtypeStruct((1, ROWS, KC), F32),
            jax.ShapeDtypeStruct((ROWS, KC), F32),
            jax.ShapeDtypeStruct((8, HALF), F32),
        ),
        in_specs=[hbm] * 5,
        out_specs=(hbm, hbm, vmem),
        scratch_shapes=[
            pltpu.VMEM((16, HALF), jnp.int32),
            pltpu.VMEM((4, 16, ROWS), jnp.int32),
            pltpu.VMEM((4, 16, ROWS), F32),
            pltpu.VMEM((16, ROWS, HALF), BF16),
            pltpu.VMEM((4, ROWS, ROWS), BF16),
            pltpu.VMEM((GROUPS, 4, 16, 32), jnp.int32),
            pltpu.VMEM((NZ, NX, TOK, HALF), BF16),
            pltpu.VMEM((NZ, 2, 2, TOK, HALF), BF16),
            pltpu.VMEM((NX, TOK, KC), BF16),
            pltpu.VMEM((HALF, NX * TOK), BF16),
            pltpu.VMEM((ROWS, 2 * TOK), BF16),
            pltpu.VMEM((ROWS + HALF, KC), F32),
            pltpu.VMEM((3, NB, NZ - 1, HALF, WIDE), jnp.int16),
            pltpu.VMEM((3, NB, NZ, HALF, WIDE), jnp.int16),
            pltpu.VMEM((3, NB, NZ - 1, 8, HALF), F32),
            pltpu.VMEM((3, NB, NZ, 8, HALF), F32),
            pltpu.VMEM((2, NB, HALF, WIDE), jnp.int16),
            pltpu.VMEM((2, NB, 8, HALF), F32),
            pltpu.VMEM((ROWS, KC), F32),
            pltpu.VMEM((ROWS, KC), F32),
            pltpu.VMEM((ROWS, KC), F32),
            pltpu.VMEM((ROWS, KC), F32),
            pltpu.VMEM((ROWS, KC), F32),
            pltpu.VMEM((ROWS, KC), F32),
            pltpu.VMEM((16, ROWS, ROWS), BF16),
            pltpu.VMEM((GROUPS, 16, HALF), F32),
            pltpu.VMEM((16, HALF), F32),
            pltpu.VMEM((16, HALF), F32),
            pltpu.VMEM((NX * NZ, 1, HALF), F32),
            pltpu.VMEM((NX * NZ, 1, HALF), F32),
            dma((NX, NZ)),
            dma((NX, NZ)),
            dma((2, NZ)),
            dma((2, NZ)),
            dma((2, NZ)),
            dma((NX,)),
            dma((NX,)),
            dma((NX,)),
            dma((NX,)),
            dma((3, NB, NZ)),
            dma((3, NB, NZ)),
            dma((3, NB, NZ)),
            dma((3, NB, NZ)),
            dma((2, NB)),
            dma((2, NB)),
            dma((GROUPS,)),
            dma((GROUPS,)),
            dma((2,)),
            dma((2,)),
            dma((3,)),
        ],
        compiler_params=pltpu.CompilerParams(
            collective_id=0, has_side_effects=True, vmem_limit_bytes=56 * 2**20),
        cost_estimate=pl.CostEstimate(flops=7 * 10**9, bytes_accessed=12 * 10**6, transcendentals=0),
    )(activations, upstream, momentum, positions, jnp.asarray(cosine_parts()))
    tile = pl.BlockSpec((STRIP, KC), lambda i: (i, 0))
    deep = pl.BlockSpec((1, STRIP, KC), lambda i: (0, i, 0))
    return pl.pallas_call(
        finish,
        grid=(ROWS // STRIP,),
        out_shape=(
            jax.ShapeDtypeStruct((1, ROWS, KC), F32),
            jax.ShapeDtypeStruct((ROWS, KC), F32),
        ),
        in_specs=[deep, tile, pl.BlockSpec((8, HALF), lambda i: (0, 0))],
        out_specs=(deep, tile),
    )(moved, comb, width)


def solution(mesh):
    placed = (
        P("dp", "fsdp", None),
        P("dp", "fsdp", None),
        P("dp", "fsdp", None),
        P(None, "fsdp", None, None),
    )
    return jax.shard_map(
        local,
        mesh=mesh,
        in_specs=placed,
        out_specs=(P("dp", "fsdp", None), P("fsdp", None)),
        check_vma=False,
    )
```
